32 devices in a mesh: groups: 2 (over y), tile: 4 (over z), chan: 2 (over x), sub: 2 (over core).
Axes of the slice: x: 2, y: 2, z: 4, core: 2. Of those that a mesh axis runs over, the one named last changes fastest.
Arguments:
- latent: bfloat16 [16, 8, 20, 512], P(('groups', 'sub'), None, 'tile', 'chan'), parts along dimension 0, may hold values from -34 to 34
- extents: int32 [4], replicated, may hold values from 1 to 4, as said below
- gain_one: float32 [512], P('chan'), may hold values from 0.1 to 1.9
- weight_one: bfloat16 [3, 3, 3, 512, 512], P(None, None, None, 'tile', 'chan'), may hold values from -0.0546875 to 0.0546875
- gain_two: float32 [512], P('chan'), may hold values from 0.1 to 1.9
- weight_two: bfloat16 [3, 3, 3, 512, 512], P(None, None, None, 'tile', 'chan'), may hold values from -0.0546875 to 0.0546875
Outputs:
- decoded: bfloat16 [16, 16, 40, 512], P(('groups', 'sub'), None, 'tile', 'chan'), parts along dimension 0
The draws below stay inside these ranges and needn't reach their ends.
There are 2 independent parts, one for each index of `groups`. The reference program is written for one: setup_inputs(seed, part) draws one part's arguments, and reference() takes and returns one part's arrays. A program takes and returns all parts, laid end to end along the dimension named above; an argument that names none is the same for every part. Nothing has to cross between parts.
Inputs may be any that keep to these rules, and one draw needn't show every extreme that they name: `extents`: entry i is how many columns of tile i + 1 tile i decodes with its own; the last entry is not used. Among the used entries, the value 4 and the value 1 both occur.
All inputs are finite; a program needn't handle non-finite values.
Results may differ from the reference program's by a relative error of at most 0.0042.
Values may be sent and summed in bfloat16 or wider, within the bound.
A program may use at most 64 MiB of HBM per device.

```python
import jax
import jax.numpy as jnp
from jax import lax

CH = 512
GROUPS = 32
ROWS = 8
TILE_W = 5
INTERSECTION = 4
FRAMES = 8
TILES = 4
COLS = 20


def draw_latent(key, part):
    keys = jax.random.split(key, 4)
    shape = (FRAMES, ROWS, COLS, CH)
    steps = jnp.arange(FRAMES).astype(jnp.float32) / (FRAMES - 1)
    frame_scale = 0.6 * jnp.power(3.0, steps) * jax.random.uniform(keys[1], (FRAMES,), jnp.float32, 0.8, 1.2)
    chan_scale = jnp.exp(jax.random.uniform(keys[2], (CH,), jnp.float32, jnp.log(0.3), jnp.log(3.0)))
    col_scale = jax.random.uniform(keys[3], (COLS,), jnp.float32, 0.7, 1.3)
    base = jnp.clip(jax.random.normal(keys[0], shape, jnp.float32), -4.0, 4.0)
    values = base * frame_scale[:, None, None, None] * col_scale[None, None, :, None] * chan_scale
    return values.astype(jnp.bfloat16)


def draw_extents(key, part):
    keys = jax.random.split(jax.random.fold_in(key, 11), 3)
    tile_ids = jnp.arange(TILES, dtype=jnp.int32)
    values = jax.random.randint(keys[0], (TILES,), 1, INTERSECTION + 1, jnp.int32)
    chosen = jax.random.randint(keys[1], (), 0, TILES - 1, jnp.int32)
    offset = jax.random.randint(keys[2], (), 0, TILES - 2, jnp.int32)
    lowest = (chosen + 1 + offset) % (TILES - 1)
    values = jnp.where(tile_ids == lowest, 1, values)
    values = jnp.where(tile_ids == chosen, INTERSECTION, values)
    return values.astype(jnp.int32)


def block_scale(stream_key, dims, pieces, least, top_value):
    def one(axis_at, blocks):
        heights = jax.random.uniform(jax.random.fold_in(jax.random.fold_in(stream_key, 6), axis_at), (blocks,), jnp.float32, least / len(pieces), top_value / len(pieces))
        return jnp.repeat(jnp.exp(heights), dims[axis_at] // blocks).reshape((-1,) + (1,) * (len(dims) - axis_at - 1))

    loudness = one(*pieces[0])
    for cut in pieces[1:]:
        loudness = loudness * one(*cut)
    return loudness


def noise(own_key, extent, width, most, cuts=(), held_as=jnp.bfloat16):
    level = block_scale(own_key, extent, cuts, -0.22, 0.18) if cuts else 1.0
    values = jax.random.normal(own_key, extent, jnp.float32) * width * level
    return jnp.minimum(jnp.maximum(values, -most), most).astype(held_as)


def setup_inputs(seed: int = 0, part: int = 0) -> dict:
    key_list = jax.random.split(jax.random.key(seed), 7)
    part_splits = jax.random.split(jax.random.fold_in(key_list[6], part), 7)
    latent = draw_latent(jax.random.fold_in(jax.random.fold_in(key_list[6], part), 71), part)
    extents = draw_extents(jax.random.fold_in(key_list[6], 71), part)
    gain_one = jnp.clip(1.0 + 0.18 * jax.random.normal(key_list[2], (CH,), jnp.float32), 0.1, 1.9)
    weight_one = noise(key_list[3], (3, 3, 3, CH, CH), (27 * CH) ** -0.5, 0.0546875, ((3, 4), (4, 2)))
    gain_two = jnp.clip(1.0 + 0.18 * jax.random.normal(key_list[4], (CH,), jnp.float32), 0.1, 1.9)
    weight_two = noise(key_list[5], (3, 3, 3, CH, CH), (27 * CH) ** -0.5, 0.0546875, ((3, 4), (4, 2)))
    return {"latent": latent, "extents": extents, "gain_one": gain_one, "weight_one": weight_one, "gain_two": gain_two, "weight_two": weight_two}


eps = 1e-06

def convolve(inputs, kernel):
    result = lax.conv_general_dilated(inputs[None], kernel, (1, 1, 1), [(0, 0), (1, 1), (1, 1)], dimension_numbers=('NDHWC', 'DHWIO', 'NDHWC'), preferred_element_type=jnp.float32)
    return result[0]

def group_norm(values, gain, count):
    group_size = CH // GROUPS
    grouped = values.reshape(values.shape[:-1] + (values.shape[-1] // group_size, group_size))
    totals = lax.optimization_barrier(jnp.sum(grouped, axis=(0, 1, 2, 4)))
    squares = lax.optimization_barrier(jnp.sum(grouped * grouped, axis=(0, 1, 2, 4)))
    size = count * group_size
    mean_val = totals / size
    variance = squares / size - mean_val * mean_val
    scaled = (grouped - mean_val[:, None]) * lax.rsqrt(variance + eps)[:, None]
    return scaled.reshape(values.shape) * gain.astype(jnp.float32)

def causal_pad(values):
    return jnp.concatenate([values[:1], values[:1], values], axis=0)

def blend_ramp(prior):
    positions = jnp.arange(2 * INTERSECTION).astype(jnp.float32) + 0.5
    limit = (2 * prior).astype(jnp.float32)[..., None]
    denom = (2 * jnp.maximum(prior, 1)).astype(jnp.float32)[..., None]
    return jnp.where(positions < limit, positions / denom, 1.0)

def decode_tile(tile_in, valid, count, gain_one, weight_one, gain_two, weight_two):
    mask = valid[None, None, :, None]
    source = tile_in.astype(jnp.float32)
    hidden = (jax.nn.silu(group_norm(source, gain_one, count)) * mask).astype(jnp.bfloat16)
    first = (convolve(causal_pad(hidden), weight_one) * mask).astype(jnp.bfloat16)
    first = lax.optimization_barrier(first)
    hidden_two = (jax.nn.silu(group_norm(first.astype(jnp.float32), gain_two, count)) * mask).astype(jnp.bfloat16)
    second = convolve(causal_pad(hidden_two), weight_two)
    return ((source + second) * mask).astype(jnp.bfloat16)

def reference(latent, extents, gain_one, weight_one, gain_two, weight_two):
    span = TILE_W + INTERSECTION
    padded = jnp.concatenate([latent, jnp.zeros((FRAMES, ROWS, INTERSECTION, CH), jnp.bfloat16)], axis=2)
    tile_ids = jnp.arange(TILES, dtype=jnp.int32)
    reaches = jnp.where(tile_ids == TILES - 1, 0, extents).astype(jnp.int32)
    columns = jnp.arange(span, dtype=jnp.int32)

    def tile_out(tile_id):
        reach = jnp.sum(jnp.where(tile_ids == tile_id, reaches, 0))
        valid = (columns < TILE_W + reach).astype(jnp.float32)
        window = lax.dynamic_slice_in_dim(padded, (tile_id * TILE_W).astype(jnp.int32), span, 2)
        window = jnp.where(valid[None, None, :, None] > 0, window, jnp.zeros_like(window))
        count = (TILE_W + reach).astype(jnp.float32) * (FRAMES * ROWS)
        return decode_tile(window, valid, count, gain_one, weight_one, gain_two, weight_two)
    decoded_tiles = lax.map(tile_out, tile_ids)
    larger = jnp.repeat(jnp.repeat(decoded_tiles, 2, axis=2), 2, axis=3)
    own = larger[:, :, :, :2 * TILE_W]
    tails = larger[:, :, :, 2 * TILE_W:]
    arrived = jnp.concatenate([jnp.zeros_like(tails[:1]), tails[:-1]], axis=0)
    prior = jnp.concatenate([jnp.zeros((1,), jnp.int32), reaches[:-1]])
    ramp = blend_ramp(prior)[:, None, None, :, None]
    head = own[:, :, :, :2 * INTERSECTION].astype(jnp.float32) * ramp + arrived.astype(jnp.float32) * (1.0 - ramp)
    joined = jnp.concatenate([head.astype(jnp.bfloat16), own[:, :, :, 2 * INTERSECTION:]], axis=3)
    return jnp.transpose(joined, (1, 2, 0, 3, 4)).reshape(FRAMES, 2 * ROWS, 2 * COLS, CH)
```

```python
import jax
import jax.numpy as jnp
from jax import lax
from jax.sharding import PartitionSpec as P

CH = 512
GROUPS = 32
INTERSECTION = 4


eps = 1e-06


def shifted(array, axis, by):
    peers = lax.axis_size(axis)
    pairs = [(i, i + by) for i in range(peers) if 0 <= i + by < peers]
    return lax.ppermute(array, axis, pairs)


def convolve(inputs, kernel):
    result = lax.conv_general_dilated(
        inputs[None],
        kernel,
        (1, 1, 1),
        [(0, 0), (1, 1), (1, 1)],
        dimension_numbers=("NDHWC", "DHWIO", "NDHWC"),
        preferred_element_type=jnp.float32,
    )
    return result[0]


def group_norm(values, gain, count):
    group_size = CH // GROUPS
    grouped = values.reshape(values.shape[:-1] + (values.shape[-1] // group_size, group_size))
    totals, squares = lax.psum(
        (jnp.sum(grouped, axis=(0, 1, 2, 4)), jnp.sum(grouped * grouped, axis=(0, 1, 2, 4))), "sub"
    )
    size = count * group_size
    mean_val = totals / size
    variance = squares / size - mean_val * mean_val
    scaled = (grouped - mean_val[:, None]) * lax.rsqrt(variance + eps)[:, None]
    return scaled.reshape(values.shape) * gain


def causal_pad(values):
    earlier = shifted(values[-2:], "sub", 1)
    repeated = jnp.concatenate([values[:1], values[:1]], axis=0)
    leading = jnp.where(lax.axis_index("sub") == 0, repeated, earlier)
    return jnp.concatenate([leading, values], axis=0)


def blend_ramp(prior):
    positions = jnp.arange(2 * INTERSECTION).astype(jnp.float32) + 0.5
    limit = (2 * prior).astype(jnp.float32)[..., None]
    denom = (2 * jnp.maximum(prior, 1)).astype(jnp.float32)[..., None]
    return jnp.where(positions < limit, positions / denom, 1.0)


def channel_conv(padded_in, weight):
    full_in = lax.all_gather(padded_in, "chan", axis=3, tiled=True)
    out_count = weight.shape[4]
    share = weight.shape[3] // lax.axis_size("sub")
    portion = lax.dynamic_slice_in_dim(weight, lax.axis_index("sub") * share, share, 3)
    fetched = lax.all_gather(portion, "tile", axis=3, tiled=True)
    sectioned = fetched.reshape(3, 3, 3, lax.axis_size("tile"), 1, share, out_count)
    whole = lax.all_gather(sectioned, "sub", axis=4, tiled=True).reshape(3, 3, 3, -1, out_count)
    return convolve(full_in, whole)


def stationary_conv(padded_in, weight):
    tiles = lax.axis_size("tile")
    share = weight.shape[3]
    full_in = lax.all_gather(padded_in, "chan", axis=3, tiled=True)
    split = full_in.reshape(full_in.shape[:3] + (tiles, share))
    mine = lax.all_to_all(split, "tile", 3, 0, tiled=False)
    partial = lax.conv_general_dilated(
        mine,
        weight,
        (1, 1, 1),
        [(0, 0), (1, 1), (1, 1)],
        dimension_numbers=("NDHWC", "DHWIO", "NDHWC"),
        preferred_element_type=jnp.float32,
    ).astype(jnp.bfloat16)
    back = lax.all_to_all(partial, "tile", 0, 0, tiled=True)
    return jnp.sum(back.astype(jnp.float32), axis=0)


def upscale(values):
    return jnp.repeat(jnp.repeat(values, 2, axis=1), 2, axis=2)


def shards(latent, extents, gain_one, weight_one, gain_two, weight_two):
    frame_count, row_count, col_count, chan_count = latent.shape
    tile_count = lax.axis_size("tile")
    conv = stationary_conv if weight_one.shape[3] % 128 == 0 else channel_conv
    place = lax.axis_index("tile")
    tile_ids = jnp.arange(tile_count, dtype=jnp.int32)
    reaches = jnp.where(tile_ids == tile_count - 1, 0, extents)
    reach = jnp.sum(jnp.where(tile_ids == place, reaches, 0))
    prior = jnp.sum(jnp.where(tile_ids == place - 1, reaches, 0))
    incoming = shifted(latent[:, :, :INTERSECTION, :], "tile", -1)
    window = jnp.concatenate([latent, incoming], axis=2)
    valid = (jnp.arange(col_count + INTERSECTION, dtype=jnp.int32) < col_count + reach).astype(
        jnp.float32
    )
    mask = valid[None, None, :, None]
    window = jnp.where(mask > 0, window, jnp.zeros_like(window))
    count = (col_count + reach).astype(jnp.float32) * (
        frame_count * lax.axis_size("sub") * row_count
    )
    source = window.astype(jnp.float32)
    hidden = (jax.nn.silu(group_norm(source, gain_one, count)) * mask).astype(jnp.bfloat16)
    first = (conv(causal_pad(hidden), weight_one) * mask).astype(jnp.bfloat16)
    first = lax.optimization_barrier(first)
    hidden_two = (
        jax.nn.silu(group_norm(first.astype(jnp.float32), gain_two, count)) * mask
    ).astype(jnp.bfloat16)
    second = conv(causal_pad(hidden_two), weight_two)
    result = ((source + second) * mask).astype(jnp.bfloat16)
    larger = upscale(result)
    own = larger[:, :, : 2 * col_count]
    arrived = shifted(larger[:, :, 2 * col_count :], "tile", 1)
    ramp = blend_ramp(prior)[None, None, :, None]
    head = own[:, :, : 2 * INTERSECTION].astype(jnp.float32) * ramp + arrived.astype(
        jnp.float32
    ) * (1.0 - ramp)
    return jnp.concatenate([head.astype(jnp.bfloat16), own[:, :, 2 * INTERSECTION :]], axis=2)


def solution(mesh):
    placed = (
        P(("groups", "sub"), None, "tile", "chan"),
        P(),
        P("chan"),
        P(None, None, None, "tile", "chan"),
        P("chan"),
        P(None, None, None, "tile", "chan"),
    )
    return jax.shard_map(
        shards,
        mesh=mesh,
        in_specs=placed,
        out_specs=P(("groups", "sub"), None, "tile", "chan"),
        check_vma=False,
    )
```

```python
import functools

import jax
import jax.numpy as jnp
from jax import lax
from jax.experimental import pallas as pl
from jax.experimental.pallas import tpu as pltpu
from jax.sharding import PartitionSpec as P

CH = 512
GROUPS = 32
INTERSECTION = 4


eps = 1e-06


def shifted(array, axis, by):
    peers = lax.axis_size(axis)
    pairs = [(i, i + by) for i in range(peers) if 0 <= i + by < peers]
    return lax.ppermute(array, axis, pairs)


def convolve(inputs, kernel):
    result = lax.conv_general_dilated(
        inputs[None],
        kernel,
        (1, 1, 1),
        [(0, 0), (1, 1), (1, 1)],
        dimension_numbers=("NDHWC", "DHWIO", "NDHWC"),
        preferred_element_type=jnp.float32,
    )
    return result[0]


def group_norm(values, gain, count):
    group_size = CH // GROUPS
    grouped = values.reshape(values.shape[:-1] + (values.shape[-1] // group_size, group_size))
    totals, squares = lax.psum(
        (jnp.sum(grouped, axis=(0, 1, 2, 4)), jnp.sum(grouped * grouped, axis=(0, 1, 2, 4))), "sub"
    )
    size = count * group_size
    mean_val = totals / size
    variance = squares / size - mean_val * mean_val
    scaled = (grouped - mean_val[:, None]) * lax.rsqrt(variance + eps)[:, None]
    return scaled.reshape(values.shape) * gain


def causal_pad(values):
    earlier = shifted(values[-2:], "sub", 1)
    repeated = jnp.concatenate([values[:1], values[:1]], axis=0)
    leading = jnp.where(lax.axis_index("sub") == 0, repeated, earlier)
    return jnp.concatenate([leading, values], axis=0)


def blend_ramp(prior):
    positions = jnp.arange(2 * INTERSECTION).astype(jnp.float32) + 0.5
    limit = (2 * prior).astype(jnp.float32)[..., None]
    denom = (2 * jnp.maximum(prior, 1)).astype(jnp.float32)[..., None]
    return jnp.where(positions < limit, positions / denom, 1.0)


def channel_conv(padded_in, weight):
    full_in = lax.all_gather(padded_in, "chan", axis=3, tiled=True)
    out_count = weight.shape[4]
    share = weight.shape[3] // lax.axis_size("sub")
    portion = lax.dynamic_slice_in_dim(weight, lax.axis_index("sub") * share, share, 3)
    fetched = lax.all_gather(portion, "tile", axis=3, tiled=True)
    sectioned = fetched.reshape(3, 3, 3, lax.axis_size("tile"), 1, share, out_count)
    whole = lax.all_gather(sectioned, "sub", axis=4, tiled=True).reshape(3, 3, 3, -1, out_count)
    return convolve(full_in, whole)


def upscale(values):
    return jnp.repeat(jnp.repeat(values, 2, axis=1), 2, axis=2)


def shards(latent, extents, gain_one, weight_one, gain_two, weight_two):
    frame_count, row_count, col_count, chan_count = latent.shape
    tile_count = lax.axis_size("tile")
    place = lax.axis_index("tile")
    tile_ids = jnp.arange(tile_count, dtype=jnp.int32)
    reaches = jnp.where(tile_ids == tile_count - 1, 0, extents)
    reach = jnp.sum(jnp.where(tile_ids == place, reaches, 0))
    prior = jnp.sum(jnp.where(tile_ids == place - 1, reaches, 0))
    incoming = shifted(latent[:, :, :INTERSECTION, :], "tile", -1)
    window = jnp.concatenate([latent, incoming], axis=2)
    valid = (jnp.arange(col_count + INTERSECTION, dtype=jnp.int32) < col_count + reach).astype(
        jnp.float32
    )
    mask = valid[None, None, :, None]
    window = jnp.where(mask > 0, window, jnp.zeros_like(window))
    count = (col_count + reach).astype(jnp.float32) * (
        frame_count * lax.axis_size("sub") * row_count
    )
    source = window.astype(jnp.float32)
    hidden = (jax.nn.silu(group_norm(source, gain_one, count)) * mask).astype(jnp.bfloat16)
    first = (channel_conv(causal_pad(hidden), weight_one) * mask).astype(jnp.bfloat16)
    first = lax.optimization_barrier(first)
    hidden_two = (
        jax.nn.silu(group_norm(first.astype(jnp.float32), gain_two, count)) * mask
    ).astype(jnp.bfloat16)
    second = channel_conv(causal_pad(hidden_two), weight_two)
    result = ((source + second) * mask).astype(jnp.bfloat16)
    larger = upscale(result)
    own = larger[:, :, : 2 * col_count]
    arrived = shifted(larger[:, :, 2 * col_count :], "tile", 1)
    ramp = blend_ramp(prior)[None, None, :, None]
    head = own[:, :, : 2 * INTERSECTION].astype(jnp.float32) * ramp + arrived.astype(
        jnp.float32
    ) * (1.0 - ramp)
    return jnp.concatenate([head.astype(jnp.bfloat16), own[:, :, 2 * INTERSECTION :]], axis=2)


MESH = pl.DeviceIdType.MESH
f32 = jnp.float32
bf16 = jnp.bfloat16


def block_kernel(dims, reach_ref, lat, gains, w_one, w_two, out, rx_one, rx_two, inc, gx, halo_one, halo_two,
                 st_own_one, st_own_two, st_sib_one, st_sib_two, xs, hs, wv_one, wv_two, tx_one, tx_two, rp_one,
                 rp_two, home, ys, tail, w_sem, dist_send, dist_recv, inc_sem, gain_send, gain_recv, halo_sem,
                 st_sem, red_send, red_recv, tail_sem):
    T, C, Q, B, F, R, KS, CL, span = dims
    FR = F * R
    pairs = T // 2
    g, z, c, s = (lax.axis_index(a) for a in ("groups", "tile", "chan", "sub"))
    sib = 1 - s
    source = z // Q
    size = CH // GROUPS

    loads = [
        pltpu.make_async_copy(w_one, wv_one, w_sem.at[0]),
        pltpu.make_async_copy(w_two, wv_two, w_sem.at[1]),
    ]
    for load in loads:
        load.start()

    def remote(src, dst, send, recv, where):
        return pltpu.make_async_remote_copy(
            src_ref=src, dst_ref=dst, send_sem=send, recv_sem=recv, device_id=where, device_id_type=MESH
        )

    barrier = pltpu.get_barrier_semaphore()
    for zz in range(T):
        for cc in range(C):
            @pl.when(jnp.logical_or(z != zz, c != cc))
            def _():
                pl.semaphore_signal(barrier, inc=1, device_id=(g, zz, cc, s), device_id_type=MESH)
    pl.semaphore_signal(barrier, inc=1, device_id=(g, z, c, sib), device_id_type=MESH)
    pl.semaphore_wait(barrier, T * C)

    def send_parts(src, rx, k, finish):
        for q in range(Q):
            for cc in range(C):
                zz = c * Q + q
                there = jnp.logical_and(z == zz, c == cc)
                move = remote(src.at[q], rx.at[z], dist_send.at[k, q * C + cc], dist_recv.at[k, z], (g, zz, cc, s))

                @pl.when(jnp.logical_not(there))
                def _():
                    if finish:
                        move.wait_send()
                    else:
                        move.start()

                if not finish:
                    @pl.when(there)
                    def _():
                        rx[z] = src[q]

    def receive_parts(src, rx, k):
        for t in range(T):
            @pl.when(jnp.logical_or(z != t, source != c))
            def _():
                remote(src.at[0], rx.at[t], dist_send.at[k, 0], dist_recv.at[k, t], (g, z, c, sib)).wait_recv()

    send_parts(lat, rx_one, 0, False)
    edge = remote(lat.at[:, 0:INTERSECTION], inc, inc_sem.at[0], inc_sem.at[1], (g, jnp.maximum(z - 1, 0), c, s))

    @pl.when(z > 0)
    def _():
        edge.start()

    @pl.when(z == T - 1)
    def _():
        inc[...] = jnp.zeros_like(inc)

    gx[c] = gains[...]
    for cc in range(C):
        @pl.when(c != cc)
        def _():
            remote(gains, gx.at[c], gain_send.at[cc], gain_recv.at[c], (g, z, cc, s)).start()

    hs[...] = jnp.zeros_like(hs)

    def reach_of(t):
        return 0 if t == T - 1 else reach_ref[t]

    my_reach = jnp.where(z == T - 1, 0, reach_ref[z])
    prior = jnp.where(z == 0, 0, reach_ref[jnp.maximum(z - 1, 0)])

    def valid(j, reach):
        return jnp.where(j < B + reach, 1.0, 0.0).astype(f32)

    def window_one(t, j):
        if j >= B:
            if t == T - 1:
                return jnp.zeros((FR, KS), f32)
            t, own, j, k = t + 1, t, j - B, j
            return rx_one[t, j].astype(f32) * valid(k, reach_of(own))
        return rx_one[t, j].astype(f32)

    def window_two(t, j):
        return rx_two[t, j].astype(f32)

    lanes = lax.broadcasted_iota(jnp.int32, (2 * T * R, KS), 1)

    def build(window, k, halo, st_own, st_sib):
        for p in range(pairs):
            total = jnp.zeros((F, 2 * R, KS), f32)
            square = jnp.zeros((F, 2 * R, KS), f32)
            for j in range(span):
                low = window(2 * p, j).reshape(F, R, KS)
                high = window(2 * p + 1, j).reshape(F, R, KS)
                both = jnp.concatenate([low, high], axis=1)
                total = total + both
                square = square + both * both
                xs[p, j] = both.astype(bf16)
            st_own[0, pl.ds(2 * p * R, 2 * R)] = jnp.sum(total, axis=0)
            st_own[1, pl.ds(2 * p * R, 2 * R)] = jnp.sum(square, axis=0)
        stats = remote(st_own, st_sib, st_sem.at[k, 0], st_sem.at[k, 1], (g, z, c, sib))
        stats.start()
        edges = remote(xs.at[:, :, F - 2:F], halo, halo_sem.at[k, 0], halo_sem.at[k, 1], (g, z, c, sib))

        @pl.when(s == 0)
        def _():
            edges.start()
            first = xs[:, :, 0:1]
            halo[:, :, 0:1] = first
            halo[:, :, 1:2] = first

        stats.wait()

        @pl.when(s == 0)
        def _():
            edges.wait_send()

        @pl.when(s == 1)
        def _():
            edges.wait_recv()

        sums = (st_own[...] + st_sib[...]).reshape(2 * T, R, KS)
        sums = jnp.broadcast_to(jnp.sum(sums, axis=1, keepdims=True), (2 * T, R, KS)).reshape(2 * T * R, KS)
        step = 1
        while step < size:
            sums = sums + jnp.where(
                (lanes & step) == 0, pltpu.roll(sums, KS - step, 1), pltpu.roll(sums, step, 1)
            )
            step *= 2
        gain = gx[source, lax.rem(z, Q)][k:k + 1]
        rows = lax.broadcasted_iota(jnp.int32, (1, R, KS), 1)
        not_first = (rows > 0).astype(f32)
        not_last = (rows < R - 1).astype(f32)
        for p in range(pairs):
            means, scales = [], []
            for t in (2 * p, 2 * p + 1):
                count = jnp.full((R, KS), (B + reach_of(t)), jnp.int32).astype(f32) * (2.0 * F * R * size)
                mean = sums[t * R:(t + 1) * R] / count
                var = sums[(T + t) * R:(T + t + 1) * R] / count - mean * mean
                means.append(mean)
                scales.append(lax.rsqrt(var + eps) * gain)
            mean = jnp.concatenate(means, axis=0)
            scale = jnp.concatenate(scales, axis=0)

            def column(j, carry):
                mask = jnp.concatenate(
                    [jnp.full((R, KS), valid(j, reach_of(t)), f32) for t in (2 * p, 2 * p + 1)], axis=0
                )
                value = jnp.concatenate([halo[p, j], xs[p, j]], axis=0).astype(f32)
                value = (value - mean) * scale
                value = value / (1.0 + jnp.exp(-value)) * mask
                hs[1, p, j + 1] = value.astype(bf16)
                split = value.reshape((F + 2) * 2, R, KS)
                down = pltpu.roll(split, 1, 1) * not_first
                hs[0, p, j + 1] = down.reshape(F + 2, 2 * R, KS).astype(bf16)
                up = pltpu.roll(split, R - 1, 1) * not_last
                hs[2, p, j + 1] = up.reshape(F + 2, 2 * R, KS).astype(bf16)
                return carry

            lax.fori_loop(0, span, column, 0)

    rows_m = span * F * 2 * R

    def convolve_reduce(wv, k, tx, rp):
        taps = [(a, b, d) for a in range(3) for b in range(3) for d in range(3)]

        def pair(p, carry):
            def patch(tap):
                a, b, d = tap
                return hs[b, p, d:d + span, a:a + F].reshape(rows_m, KS)

            acc = None
            for at in range(0, len(taps), 2):
                chosen = taps[at:at + 2]
                lhs = jnp.concatenate([patch(tap) for tap in chosen], axis=1)
                term = jnp.dot(lhs, wv[at * KS:(at + len(chosen)) * KS], preferred_element_type=f32)
                acc = term if acc is None else acc + term
            acc = acc.reshape(span * F, 2 * R, CL)
            for h in range(2):
                t = 2 * p + h
                tx[t] = acc[:, h * R:(h + 1) * R].reshape(span * FR, CL).astype(bf16)

                @pl.when(t != z)
                def _():
                    remote(tx.at[t], rp.at[z], red_send.at[k, t], red_recv.at[k, z], (g, t, c, s)).start()

            return carry

        lax.fori_loop(0, pairs, pair, 0)
        rp[z] = tx[z]
        for t in range(T):
            @pl.when(z != t)
            def _():
                move = remote(tx.at[t], rp.at[t], red_send.at[k, t], red_recv.at[k, t], (g, t, c, s))
                move.wait_send()
                move.wait_recv()

    def summed(rp, j):
        total = rp[0, j * FR:(j + 1) * FR].astype(f32)
        for t in range(1, T):
            total = total + rp[t, j * FR:(j + 1) * FR].astype(f32)
        return total

    receive_parts(lat, rx_one, 0)
    for cc in range(C):
        @pl.when(c != cc)
        def _():
            move = remote(gains, gx.at[cc], gain_send.at[cc], gain_recv.at[cc], (g, z, cc, s))
            move.wait_send()
            move.wait_recv()
    build(window_one, 0, halo_one, st_own_one, st_sib_one)
    loads[0].wait()
    convolve_reduce(wv_one, 0, tx_one, rp_one)
    for j in range(span):
        row = (summed(rp_one, j) * valid(j, my_reach)).astype(bf16)
        for q in range(Q):
            home[q, j] = row[:, q * KS:(q + 1) * KS]
    send_parts(home, rx_two, 1, False)
    receive_parts(home, rx_two, 1)
    build(window_two, 1, halo_two, st_own_two, st_sib_two)
    loads[1].wait()
    convolve_reduce(wv_two, 1, tx_two, rp_two)

    @pl.when(z > 0)
    def _():
        edge.wait_send()

    @pl.when(z < T - 1)
    def _():
        edge.wait_recv()

    send_parts(lat, rx_one, 0, True)
    send_parts(home, rx_two, 1, True)
    for j in reversed(range(span)):
        row = summed(rp_two, j)
        for q in range(Q):
            base = lat[q, j] if j < B else inc[q, j - B]
            ys[q, j] = ((base.astype(f32) + row[:, q * KS:(q + 1) * KS]) * valid(j, my_reach)).astype(bf16)
    spill = remote(
        ys.at[:, B:span], tail, tail_sem.at[0], tail_sem.at[1], (g, jnp.minimum(z + 1, T - 1), c, s)
    )

    @pl.when(z < T - 1)
    def _():
        spill.start()

    @pl.when(z == 0)
    def _():
        tail[...] = jnp.zeros_like(tail)

    @pl.when(z > 0)
    def _():
        spill.wait_recv()

    for j in range(2 * B):
        if j < 2 * INTERSECTION:
            limit = jnp.full((FR, KS), 2 * prior, jnp.int32).astype(f32)
            spot = jnp.full((FR, KS), j + 0.5, f32)
            ramp = jnp.where(spot < limit, spot / jnp.maximum(limit, 2.0), 1.0)
            for q in range(Q):
                mixed = ys[q, j // 2].astype(f32) * ramp + tail[q, j // 2].astype(f32) * (1.0 - ramp)
                out[q, j] = mixed.astype(bf16)
        else:
            for q in range(Q):
                out[q, j] = ys[q, j // 2]

    @pl.when(z < T - 1)
    def _():
        spill.wait_send()


def stationary(latent, extents, gain_one, weight_one, gain_two, weight_two):
    F, R, B, CL = latent.shape
    T, C = lax.axis_size("tile"), lax.axis_size("chan")
    KS = weight_one.shape[3]
    Q = CL // KS
    span = B + INTERSECTION
    FR = F * R
    pairs = T // 2
    lat = latent.reshape(FR, B, Q, KS).transpose(2, 1, 0, 3)
    gains = jnp.stack([gain_one.reshape(Q, KS), gain_two.reshape(Q, KS)], axis=1)
    gains = jnp.pad(gains, ((0, 0), (0, 6), (0, 0)))
    taps = weight_one.shape[0] * weight_one.shape[1] * weight_one.shape[2]
    w_one = weight_one.reshape(taps * KS, CL)
    w_two = weight_two.reshape(taps * KS, CL)
    vm = pltpu.VMEM
    dma = pltpu.SemaphoreType.DMA
    scratch = [
        vm((T, B, FR, KS), bf16), vm((T, span, FR, KS), bf16), vm((Q, INTERSECTION, FR, KS), bf16),
        vm((C, Q, 8, KS), f32),
        vm((pairs, span, 2, 2 * R, KS), bf16), vm((pairs, span, 2, 2 * R, KS), bf16),
        vm((2, T * R, KS), f32), vm((2, T * R, KS), f32), vm((2, T * R, KS), f32), vm((2, T * R, KS), f32),
        vm((pairs, span, F, 2 * R, KS), bf16), vm((3, pairs, span + 2, F + 2, 2 * R, KS), bf16),
        vm(w_one.shape, bf16), vm(w_two.shape, bf16),
        vm((T, span * FR, CL), bf16), vm((T, span * FR, CL), bf16),
        vm((T, span * FR, CL), bf16), vm((T, span * FR, CL), bf16),
        vm((Q, span, FR, KS), bf16), vm((Q, span, FR, KS), bf16), vm((Q, INTERSECTION, FR, KS), bf16),
        dma((2,)), dma((2, Q * C)), dma((2, T)), dma((2,)), dma((C,)), dma((C,)), dma((2, 2)), dma((2, 2)),
        dma((2, T)), dma((2, T)), dma((2,)),
    ]
    whole = pl.BlockSpec(memory_space=pltpu.VMEM)
    result = pl.pallas_call(
        functools.partial(block_kernel, (T, C, Q, B, F, R, KS, CL, span)),
        out_shape=jax.ShapeDtypeStruct((Q, 2 * B, FR, KS), bf16),
        in_specs=[pl.BlockSpec(memory_space=pltpu.SMEM), whole, whole,
                  pl.BlockSpec(memory_space=pl.ANY), pl.BlockSpec(memory_space=pl.ANY)],
        out_specs=whole,
        scratch_shapes=scratch,
        compiler_params=pltpu.CompilerParams(
            collective_id=0, has_side_effects=True, vmem_limit_bytes=48 * 1024 * 1024
        ),
    )(extents, lat, gains, w_one, w_two)
    result = result.reshape(Q, 2 * B, F, R, KS).transpose(2, 3, 1, 0, 4).reshape(F, R, 2 * B, CL)
    return jnp.repeat(result, 2, axis=1)


def choose(latent, extents, gain_one, weight_one, gain_two, weight_two):
    frames, rows, cols, chans = latent.shape
    share = weight_one.shape[3]
    fits = (
        share % 128 == 0
        and chans % share == 0
        and lax.axis_size("tile") % 2 == 0
        and lax.axis_size("sub") == 2
        and rows == 8
        and frames >= 2
        and (frames * rows) % 16 == 0
        and cols >= INTERSECTION
    )
    plan = stationary if fits else shards
    return plan(latent, extents, gain_one, weight_one, gain_two, weight_two)


def solution(mesh):
    placed = (
        P(("groups", "sub"), None, "tile", "chan"),
        P(),
        P("chan"),
        P(None, None, None, "tile", "chan"),
        P("chan"),
        P(None, None, None, "tile", "chan"),
    )
    return jax.shard_map(
        choose,
        mesh=mesh,
        in_specs=placed,
        out_specs=P(("groups", "sub"), None, "tile", "chan"),
        check_vma=False,
    )
```

```python
import functools

import jax
import jax.numpy as jnp
from jax import lax
from jax.experimental import pallas as pl
from jax.experimental.pallas import tpu as pltpu
from jax.sharding import PartitionSpec as P

CH = 512
GROUPS = 32
INTERSECTION = 4


eps = 1e-06


def shifted(array, axis, by):
    peers = lax.axis_size(axis)
    pairs = [(i, i + by) for i in range(peers) if 0 <= i + by < peers]
    return lax.ppermute(array, axis, pairs)


def convolve(inputs, kernel):
    result = lax.conv_general_dilated(
        inputs[None],
        kernel,
        (1, 1, 1),
        [(0, 0), (1, 1), (1, 1)],
        dimension_numbers=("NDHWC", "DHWIO", "NDHWC"),
        preferred_element_type=jnp.float32,
    )
    return result[0]


def group_norm(values, gain, count):
    group_size = CH // GROUPS
    grouped = values.reshape(values.shape[:-1] + (values.shape[-1] // group_size, group_size))
    totals, squares = lax.psum(
        (jnp.sum(grouped, axis=(0, 1, 2, 4)), jnp.sum(grouped * grouped, axis=(0, 1, 2, 4))), "sub"
    )
    size = count * group_size
    mean_val = totals / size
    variance = squares / size - mean_val * mean_val
    scaled = (grouped - mean_val[:, None]) * lax.rsqrt(variance + eps)[:, None]
    return scaled.reshape(values.shape) * gain


def causal_pad(values):
    earlier = shifted(values[-2:], "sub", 1)
    repeated = jnp.concatenate([values[:1], values[:1]], axis=0)
    leading = jnp.where(lax.axis_index("sub") == 0, repeated, earlier)
    return jnp.concatenate([leading, values], axis=0)


def blend_ramp(prior):
    positions = jnp.arange(2 * INTERSECTION).astype(jnp.float32) + 0.5
    limit = (2 * prior).astype(jnp.float32)[..., None]
    denom = (2 * jnp.maximum(prior, 1)).astype(jnp.float32)[..., None]
    return jnp.where(positions < limit, positions / denom, 1.0)


def channel_conv(padded_in, weight):
    full_in = lax.all_gather(padded_in, "chan", axis=3, tiled=True)
    out_count = weight.shape[4]
    share = weight.shape[3] // lax.axis_size("sub")
    portion = lax.dynamic_slice_in_dim(weight, lax.axis_index("sub") * share, share, 3)
    fetched = lax.all_gather(portion, "tile", axis=3, tiled=True)
    sectioned = fetched.reshape(3, 3, 3, lax.axis_size("tile"), 1, share, out_count)
    whole = lax.all_gather(sectioned, "sub", axis=4, tiled=True).reshape(3, 3, 3, -1, out_count)
    return convolve(full_in, whole)


def upscale(values):
    return jnp.repeat(jnp.repeat(values, 2, axis=1), 2, axis=2)


def shards(latent, extents, gain_one, weight_one, gain_two, weight_two):
    frame_count, row_count, col_count, chan_count = latent.shape
    tile_count = lax.axis_size("tile")
    place = lax.axis_index("tile")
    tile_ids = jnp.arange(tile_count, dtype=jnp.int32)
    reaches = jnp.where(tile_ids == tile_count - 1, 0, extents)
    reach = jnp.sum(jnp.where(tile_ids == place, reaches, 0))
    prior = jnp.sum(jnp.where(tile_ids == place - 1, reaches, 0))
    incoming = shifted(latent[:, :, :INTERSECTION, :], "tile", -1)
    window = jnp.concatenate([latent, incoming], axis=2)
    valid = (jnp.arange(col_count + INTERSECTION, dtype=jnp.int32) < col_count + reach).astype(
        jnp.float32
    )
    mask = valid[None, None, :, None]
    window = jnp.where(mask > 0, window, jnp.zeros_like(window))
    count = (col_count + reach).astype(jnp.float32) * (
        frame_count * lax.axis_size("sub") * row_count
    )
    source = window.astype(jnp.float32)
    hidden = (jax.nn.silu(group_norm(source, gain_one, count)) * mask).astype(jnp.bfloat16)
    first = (channel_conv(causal_pad(hidden), weight_one) * mask).astype(jnp.bfloat16)
    first = lax.optimization_barrier(first)
    hidden_two = (
        jax.nn.silu(group_norm(first.astype(jnp.float32), gain_two, count)) * mask
    ).astype(jnp.bfloat16)
    second = channel_conv(causal_pad(hidden_two), weight_two)
    result = ((source + second) * mask).astype(jnp.bfloat16)
    larger = upscale(result)
    own = larger[:, :, : 2 * col_count]
    arrived = shifted(larger[:, :, 2 * col_count :], "tile", 1)
    ramp = blend_ramp(prior)[None, None, :, None]
    head = own[:, :, : 2 * INTERSECTION].astype(jnp.float32) * ramp + arrived.astype(
        jnp.float32
    ) * (1.0 - ramp)
    return jnp.concatenate([head.astype(jnp.bfloat16), own[:, :, 2 * INTERSECTION :]], axis=2)


MESH = pl.DeviceIdType.MESH
f32 = jnp.float32
bf16 = jnp.bfloat16


def block_kernel(dims, reach_ref, lat, gains, w_one, w_two, out, rx_one, rx_two, inc, gx, halo_one, halo_two,
                 st_own_one, st_own_two, st_sib_one, st_sib_two, xs, hs, wv_one, wv_two, tx_one, tx_two, near_one,
                 near_two, rp_one, rp_two, home, ys, tail, w_sem, dist_send, dist_recv, fwd_send, inc_sem, gain_send, gain_recv, halo_sem,
                 st_sem, red_send, red_recv, tail_sem):
    T, C, Q, B, F, R, KS, CL, span = dims
    FR = F * R
    pairs = T // 2
    g, z, c, s = (lax.axis_index(a) for a in ("groups", "tile", "chan", "sub"))
    sib = 1 - s
    source = z // Q
    block, odd = z // 2, lax.rem(z, 2)
    partner = z + 1 - 2 * odd
    size = CH // GROUPS

    loads = [
        pltpu.make_async_copy(w_one, wv_one, w_sem.at[0]),
        pltpu.make_async_copy(w_two, wv_two, w_sem.at[1]),
    ]
    for load in loads:
        load.start()

    def remote(src, dst, send, recv, where):
        return pltpu.make_async_remote_copy(
            src_ref=src, dst_ref=dst, send_sem=send, recv_sem=recv, device_id=where, device_id_type=MESH
        )

    barrier = pltpu.get_barrier_semaphore()
    for zz in range(T):
        for cc in range(C):
            @pl.when(jnp.logical_or(z != zz, c != cc))
            def _():
                pl.semaphore_signal(barrier, inc=1, device_id=(g, zz, cc, s), device_id_type=MESH)
    pl.semaphore_signal(barrier, inc=1, device_id=(g, z, c, sib), device_id_type=MESH)
    pl.semaphore_wait(barrier, T * C)

    def send_parts(src, rx, k, finish):
        for q in range(Q):
            zz = c * Q + q
            move = remote(src.at[q], rx.at[z], dist_send.at[k, q], dist_recv.at[k, z], (g, zz, c, s))

            @pl.when(z != zz)
            def _():
                if finish:
                    move.wait_send()
                else:
                    move.start()

            if not finish:
                @pl.when(z == zz)
                def _():
                    rx[z] = src[q]
        if finish:
            @pl.when(source == c)
            def _():
                for t in range(T):
                    for off in range(1, C):
                        onward(rx, k, t, off).wait_send()

    def onward(rx, k, t, off):
        there = (g, z, lax.rem(c + off, C), s)
        return remote(rx.at[t], rx.at[t], fwd_send.at[k, off, t], dist_recv.at[k, t], there)

    def receive_parts(src, rx, k):
        steps = [0]
        for far in range(1, T):
            steps += [far, -far]
        for far in steps:
            t = z + far

            @pl.when(jnp.logical_and(t >= 0, t < T))
            def _():
                arrival = remote(src.at[0], rx.at[t], dist_send.at[k, 0], dist_recv.at[k, t], (g, z, c, sib))

                @pl.when(source == c)
                def _():
                    if far != 0:
                        arrival.wait_recv()
                    for off in range(1, C):
                        onward(rx, k, t, off).start()

        @pl.when(source != c)
        def _():
            for t in range(T):
                remote(src.at[0], rx.at[t], dist_send.at[k, 0], dist_recv.at[k, t], (g, z, c, sib)).wait_recv()

    send_parts(lat, rx_one, 0, False)
    edge = remote(lat.at[:, 0:INTERSECTION], inc, inc_sem.at[0], inc_sem.at[1], (g, jnp.maximum(z - 1, 0), c, s))

    @pl.when(z > 0)
    def _():
        edge.start()

    @pl.when(z == T - 1)
    def _():
        inc[...] = jnp.zeros_like(inc)

    gx[c] = gains[...]
    for cc in range(C):
        @pl.when(c != cc)
        def _():
            remote(gains, gx.at[c], gain_send.at[cc], gain_recv.at[c], (g, z, cc, s)).start()

    hs[...] = jnp.zeros_like(hs)

    def reach_of(t):
        return 0 if t == T - 1 else reach_ref[t]

    my_reach = jnp.where(z == T - 1, 0, reach_ref[z])
    prior = jnp.where(z == 0, 0, reach_ref[jnp.maximum(z - 1, 0)])

    def valid(j, reach):
        return jnp.where(j < B + reach, 1.0, 0.0).astype(f32)

    def window_one(t, j):
        if j >= B:
            if t == T - 1:
                return jnp.zeros((FR, KS), f32)
            t, own, j, k = t + 1, t, j - B, j
            return rx_one[t, j].astype(f32) * valid(k, reach_of(own))
        return rx_one[t, j].astype(f32)

    def window_two(t, j):
        return rx_two[t, j].astype(f32)

    lanes = lax.broadcasted_iota(jnp.int32, (2 * T * R, KS), 1)

    def build(window, k, halo, st_own, st_sib):
        for p in range(pairs):
            total = jnp.zeros((F, 2 * R, KS), f32)
            square = jnp.zeros((F, 2 * R, KS), f32)
            for j in range(span):
                low = window(2 * p, j).reshape(F, R, KS)
                high = window(2 * p + 1, j).reshape(F, R, KS)
                both = jnp.concatenate([low, high], axis=1)
                total = total + both
                square = square + both * both
                xs[p, j] = both.astype(bf16)
            st_own[0, pl.ds(2 * p * R, 2 * R)] = jnp.sum(total, axis=0)
            st_own[1, pl.ds(2 * p * R, 2 * R)] = jnp.sum(square, axis=0)
        stats = remote(st_own, st_sib, st_sem.at[k, 0], st_sem.at[k, 1], (g, z, c, sib))
        stats.start()
        edges = remote(xs.at[:, :, F - 2:F], halo, halo_sem.at[k, 0], halo_sem.at[k, 1], (g, z, c, sib))

        @pl.when(s == 0)
        def _():
            edges.start()
            first = xs[:, :, 0:1]
            halo[:, :, 0:1] = first
            halo[:, :, 1:2] = first

        stats.wait()

        @pl.when(s == 0)
        def _():
            edges.wait_send()

        @pl.when(s == 1)
        def _():
            edges.wait_recv()

        sums = (st_own[...] + st_sib[...]).reshape(2 * T, R, KS)
        sums = jnp.broadcast_to(jnp.sum(sums, axis=1, keepdims=True), (2 * T, R, KS)).reshape(2 * T * R, KS)
        step = 1
        while step < size:
            sums = sums + jnp.where(
                (lanes & step) == 0, pltpu.roll(sums, KS - step, 1), pltpu.roll(sums, step, 1)
            )
            step *= 2
        gain = gx[source, lax.rem(z, Q)][k:k + 1]
        rows = lax.broadcasted_iota(jnp.int32, (1, R, KS), 1)
        not_first = (rows > 0).astype(f32)
        not_last = (rows < R - 1).astype(f32)
        for p in range(pairs):
            means, scales = [], []
            for t in (2 * p, 2 * p + 1):
                count = jnp.full((R, KS), (B + reach_of(t)), jnp.int32).astype(f32) * (2.0 * F * R * size)
                mean = sums[t * R:(t + 1) * R] / count
                var = sums[(T + t) * R:(T + t + 1) * R] / count - mean * mean
                means.append(mean)
                scales.append(lax.rsqrt(var + eps) * gain)
            mean = jnp.concatenate(means, axis=0)
            scale = jnp.concatenate(scales, axis=0)

            def column(j, carry):
                mask = jnp.concatenate(
                    [jnp.full((R, KS), valid(j, reach_of(t)), f32) for t in (2 * p, 2 * p + 1)], axis=0
                )
                value = jnp.concatenate([halo[p, j], xs[p, j]], axis=0).astype(f32)
                value = (value - mean) * scale
                value = value / (1.0 + jnp.exp(-value)) * mask
                hs[1, p, j + 1] = value.astype(bf16)
                split = value.reshape((F + 2) * 2, R, KS)
                down = pltpu.roll(split, 1, 1) * not_first
                hs[0, p, j + 1] = down.reshape(F + 2, 2 * R, KS).astype(bf16)
                up = pltpu.roll(split, R - 1, 1) * not_last
                hs[2, p, j + 1] = up.reshape(F + 2, 2 * R, KS).astype(bf16)
                return carry

            lax.fori_loop(0, span, column, 0)

    rows_m = span * F * 2 * R

    def convolve_reduce(wv, k, tx, near, rp):
        taps = [(a, b, d) for a in range(3) for b in range(3) for d in range(3)]

        def pair(i, carry):
            p = lax.rem(block + 1 + i, pairs)

            def patch(tap):
                a, b, d = tap
                return hs[b, p, d:d + span, a:a + F].reshape(rows_m, KS)

            acc = None
            for at in range(0, len(taps), 2):
                chosen = taps[at:at + 2]
                lhs = jnp.concatenate([patch(tap) for tap in chosen], axis=1)
                term = jnp.dot(lhs, wv[at * KS:(at + len(chosen)) * KS], preferred_element_type=f32)
                acc = term if acc is None else acc + term
            acc = acc.reshape(span * F, 2 * R, CL)
            for h in range(2):
                tx[2 * p + h] = acc[:, h * R:(h + 1) * R].reshape(span * FR, CL).astype(bf16)
            handed(p).start()
            return carry

        def handed(p):
            return remote(
                tx.at[2 * p + 1 - odd], near.at[p], red_send.at[k, p], red_recv.at[k, p], (g, partner, c, s)
            )

        def combined(p):
            t = 2 * p + odd
            return remote(
                tx.at[t], rp.at[block], red_send.at[k, pairs + p], red_recv.at[k, pairs + block], (g, t, c, s)
            )

        lax.fori_loop(0, pairs, pair, 0)
        rp[block] = tx[z]
        for i in range(pairs):
            p = lax.rem(block + 1 + i, pairs)
            handed(p).wait_recv()
            if i < pairs - 1:
                t = 2 * p + odd
                tx[t] = (tx[t].astype(f32) + near[p].astype(f32)).astype(bf16)
                combined(p).start()
        for i in range(pairs):
            p = lax.rem(block + 1 + i, pairs)
            handed(p).wait_send()
            if i < pairs - 1:
                combined(p).wait_send()
                remote(
                    tx.at[z], rp.at[p], red_send.at[k, pairs + p], red_recv.at[k, pairs + p], (g, partner, c, s)
                ).wait_recv()

    def summed(near, rp, j):
        total = near[block, j * FR:(j + 1) * FR].astype(f32)
        for m in range(pairs):
            total = total + rp[m, j * FR:(j + 1) * FR].astype(f32)
        return total

    receive_parts(lat, rx_one, 0)
    for cc in range(C):
        @pl.when(c != cc)
        def _():
            move = remote(gains, gx.at[cc], gain_send.at[cc], gain_recv.at[cc], (g, z, cc, s))
            move.wait_send()
            move.wait_recv()
    build(window_one, 0, halo_one, st_own_one, st_sib_one)
    loads[0].wait()
    convolve_reduce(wv_one, 0, tx_one, near_one, rp_one)
    for j in range(span):
        row = (summed(near_one, rp_one, j) * valid(j, my_reach)).astype(bf16)
        for q in range(Q):
            home[q, j] = row[:, q * KS:(q + 1) * KS]
    send_parts(home, rx_two, 1, False)
    receive_parts(home, rx_two, 1)
    build(window_two, 1, halo_two, st_own_two, st_sib_two)
    loads[1].wait()
    convolve_reduce(wv_two, 1, tx_two, near_two, rp_two)

    @pl.when(z > 0)
    def _():
        edge.wait_send()

    @pl.when(z < T - 1)
    def _():
        edge.wait_recv()

    send_parts(lat, rx_one, 0, True)
    send_parts(home, rx_two, 1, True)
    for j in reversed(range(span)):
        row = summed(near_two, rp_two, j)
        for q in range(Q):
            base = lat[q, j] if j < B else inc[q, j - B]
            ys[q, j] = ((base.astype(f32) + row[:, q * KS:(q + 1) * KS]) * valid(j, my_reach)).astype(bf16)
    spill = remote(
        ys.at[:, B:span], tail, tail_sem.at[0], tail_sem.at[1], (g, jnp.minimum(z + 1, T - 1), c, s)
    )

    @pl.when(z < T - 1)
    def _():
        spill.start()

    @pl.when(z == 0)
    def _():
        tail[...] = jnp.zeros_like(tail)

    @pl.when(z > 0)
    def _():
        spill.wait_recv()

    for j in range(2 * B):
        if j < 2 * INTERSECTION:
            limit = jnp.full((FR, KS), 2 * prior, jnp.int32).astype(f32)
            spot = jnp.full((FR, KS), j + 0.5, f32)
            ramp = jnp.where(spot < limit, spot / jnp.maximum(limit, 2.0), 1.0)
            for q in range(Q):
                mixed = ys[q, j // 2].astype(f32) * ramp + tail[q, j // 2].astype(f32) * (1.0 - ramp)
                out[q, j] = mixed.astype(bf16)
        else:
            for q in range(Q):
                out[q, j] = ys[q, j // 2]

    @pl.when(z < T - 1)
    def _():
        spill.wait_send()


def stationary(latent, extents, gain_one, weight_one, gain_two, weight_two):
    F, R, B, CL = latent.shape
    T, C = lax.axis_size("tile"), lax.axis_size("chan")
    KS = weight_one.shape[3]
    Q = CL // KS
    span = B + INTERSECTION
    FR = F * R
    pairs = T // 2
    lat = latent.reshape(FR, B, Q, KS).transpose(2, 1, 0, 3)
    gains = jnp.stack([gain_one.reshape(Q, KS), gain_two.reshape(Q, KS)], axis=1)
    gains = jnp.pad(gains, ((0, 0), (0, 6), (0, 0)))
    taps = weight_one.shape[0] * weight_one.shape[1] * weight_one.shape[2]
    w_one = weight_one.reshape(taps * KS, CL)
    w_two = weight_two.reshape(taps * KS, CL)
    vm = pltpu.VMEM
    dma = pltpu.SemaphoreType.DMA
    scratch = [
        vm((T, B, FR, KS), bf16), vm((T, span, FR, KS), bf16), vm((Q, INTERSECTION, FR, KS), bf16),
        vm((C, Q, 8, KS), f32),
        vm((pairs, span, 2, 2 * R, KS), bf16), vm((pairs, span, 2, 2 * R, KS), bf16),
        vm((2, T * R, KS), f32), vm((2, T * R, KS), f32), vm((2, T * R, KS), f32), vm((2, T * R, KS), f32),
        vm((pairs, span, F, 2 * R, KS), bf16), vm((3, pairs, span + 2, F + 2, 2 * R, KS), bf16),
        vm(w_one.shape, bf16), vm(w_two.shape, bf16),
        vm((T, span * FR, CL), bf16), vm((T, span * FR, CL), bf16),
        vm((pairs, span * FR, CL), bf16), vm((pairs, span * FR, CL), bf16),
        vm((pairs, span * FR, CL), bf16), vm((pairs, span * FR, CL), bf16),
        vm((Q, span, FR, KS), bf16), vm((Q, span, FR, KS), bf16), vm((Q, INTERSECTION, FR, KS), bf16),
        dma((2,)), dma((2, Q)), dma((2, T)), dma((2, C, T)), dma((2,)), dma((C,)), dma((C,)), dma((2, 2)), dma((2, 2)),
        dma((2, T)), dma((2, T)), dma((2,)),
    ]
    whole = pl.BlockSpec(memory_space=pltpu.VMEM)
    result = pl.pallas_call(
        functools.partial(block_kernel, (T, C, Q, B, F, R, KS, CL, span)),
        out_shape=jax.ShapeDtypeStruct((Q, 2 * B, FR, KS), bf16),
        in_specs=[pl.BlockSpec(memory_space=pltpu.SMEM), whole, whole,
                  pl.BlockSpec(memory_space=pl.ANY), pl.BlockSpec(memory_space=pl.ANY)],
        out_specs=whole,
        scratch_shapes=scratch,
        compiler_params=pltpu.CompilerParams(
            collective_id=0, has_side_effects=True, vmem_limit_bytes=60 * 1024 * 1024
        ),
    )(extents, lat, gains, w_one, w_two)
    result = result.reshape(Q, 2 * B, F, R, KS).transpose(2, 3, 1, 0, 4).reshape(F, R, 2 * B, CL)
    return jnp.repeat(result, 2, axis=1)


def choose(latent, extents, gain_one, weight_one, gain_two, weight_two):
    frames, rows, cols, chans = latent.shape
    share = weight_one.shape[3]
    fits = (
        share % 128 == 0
        and chans % share == 0
        and lax.axis_size("tile") % 2 == 0
        and lax.axis_size("sub") == 2
        and rows == 8
        and frames >= 2
        and (frames * rows) % 16 == 0
        and cols >= INTERSECTION
    )
    plan = stationary if fits else shards
    return plan(latent, extents, gain_one, weight_one, gain_two, weight_two)


def solution(mesh):
    placed = (
        P(("groups", "sub"), None, "tile", "chan"),
        P(),
        P("chan"),
        P(None, None, None, "tile", "chan"),
        P("chan"),
        P(None, None, None, "tile", "chan"),
    )
    return jax.shard_map(
        choose,
        mesh=mesh,
        in_specs=placed,
        out_specs=P(("groups", "sub"), None, "tile", "chan"),
        check_vma=False,
    )
```

```python
import functools

import jax
import jax.numpy as jnp
from jax import lax
from jax.experimental import pallas as pl
from jax.experimental.pallas import tpu as pltpu
from jax.sharding import PartitionSpec as P

CH = 512
GROUPS = 32
INTERSECTION = 4


eps = 1e-06


def shifted(array, axis, by):
    peers = lax.axis_size(axis)
    pairs = [(i, i + by) for i in range(peers) if 0 <= i + by < peers]
    return lax.ppermute(array, axis, pairs)


def convolve(inputs, kernel):
    result = lax.conv_general_dilated(
        inputs[None],
        kernel,
        (1, 1, 1),
        [(0, 0), (1, 1), (1, 1)],
        dimension_numbers=("NDHWC", "DHWIO", "NDHWC"),
        preferred_element_type=jnp.float32,
    )
    return result[0]


def group_norm(values, gain, count):
    group_size = CH // GROUPS
    grouped = values.reshape(values.shape[:-1] + (values.shape[-1] // group_size, group_size))
    totals, squares = lax.psum(
        (jnp.sum(grouped, axis=(0, 1, 2, 4)), jnp.sum(grouped * grouped, axis=(0, 1, 2, 4))), "sub"
    )
    size = count * group_size
    mean_val = totals / size
    variance = squares / size - mean_val * mean_val
    scaled = (grouped - mean_val[:, None]) * lax.rsqrt(variance + eps)[:, None]
    return scaled.reshape(values.shape) * gain


def causal_pad(values):
    earlier = shifted(values[-2:], "sub", 1)
    repeated = jnp.concatenate([values[:1], values[:1]], axis=0)
    leading = jnp.where(lax.axis_index("sub") == 0, repeated, earlier)
    return jnp.concatenate([leading, values], axis=0)


def blend_ramp(prior):
    positions = jnp.arange(2 * INTERSECTION).astype(jnp.float32) + 0.5
    limit = (2 * prior).astype(jnp.float32)[..., None]
    denom = (2 * jnp.maximum(prior, 1)).astype(jnp.float32)[..., None]
    return jnp.where(positions < limit, positions / denom, 1.0)


def channel_conv(padded_in, weight):
    full_in = lax.all_gather(padded_in, "chan", axis=3, tiled=True)
    out_count = weight.shape[4]
    share = weight.shape[3] // lax.axis_size("sub")
    portion = lax.dynamic_slice_in_dim(weight, lax.axis_index("sub") * share, share, 3)
    fetched = lax.all_gather(portion, "tile", axis=3, tiled=True)
    sectioned = fetched.reshape(3, 3, 3, lax.axis_size("tile"), 1, share, out_count)
    whole = lax.all_gather(sectioned, "sub", axis=4, tiled=True).reshape(3, 3, 3, -1, out_count)
    return convolve(full_in, whole)


def upscale(values):
    return jnp.repeat(jnp.repeat(values, 2, axis=1), 2, axis=2)


def shards(latent, extents, gain_one, weight_one, gain_two, weight_two):
    frame_count, row_count, col_count, chan_count = latent.shape
    tile_count = lax.axis_size("tile")
    place = lax.axis_index("tile")
    tile_ids = jnp.arange(tile_count, dtype=jnp.int32)
    reaches = jnp.where(tile_ids == tile_count - 1, 0, extents)
    reach = jnp.sum(jnp.where(tile_ids == place, reaches, 0))
    prior = jnp.sum(jnp.where(tile_ids == place - 1, reaches, 0))
    incoming = shifted(latent[:, :, :INTERSECTION, :], "tile", -1)
    window = jnp.concatenate([latent, incoming], axis=2)
    valid = (jnp.arange(col_count + INTERSECTION, dtype=jnp.int32) < col_count + reach).astype(
        jnp.float32
    )
    mask = valid[None, None, :, None]
    window = jnp.where(mask > 0, window, jnp.zeros_like(window))
    count = (col_count + reach).astype(jnp.float32) * (
        frame_count * lax.axis_size("sub") * row_count
    )
    source = window.astype(jnp.float32)
    hidden = (jax.nn.silu(group_norm(source, gain_one, count)) * mask).astype(jnp.bfloat16)
    first = (channel_conv(causal_pad(hidden), weight_one) * mask).astype(jnp.bfloat16)
    first = lax.optimization_barrier(first)
    hidden_two = (
        jax.nn.silu(group_norm(first.astype(jnp.float32), gain_two, count)) * mask
    ).astype(jnp.bfloat16)
    second = channel_conv(causal_pad(hidden_two), weight_two)
    result = ((source + second) * mask).astype(jnp.bfloat16)
    larger = upscale(result)
    own = larger[:, :, : 2 * col_count]
    arrived = shifted(larger[:, :, 2 * col_count :], "tile", 1)
    ramp = blend_ramp(prior)[None, None, :, None]
    head = own[:, :, : 2 * INTERSECTION].astype(jnp.float32) * ramp + arrived.astype(
        jnp.float32
    ) * (1.0 - ramp)
    return jnp.concatenate([head.astype(jnp.bfloat16), own[:, :, 2 * INTERSECTION :]], axis=2)


MESH = pl.DeviceIdType.MESH
f32 = jnp.float32
bf16 = jnp.bfloat16


def block_kernel(dims, reach_ref, lat, gains, w_one, w_two, out, rx_one, rx_two, inc, gx, halo_one, halo_two,
                 st_own_one, st_own_two, st_sib_one, st_sib_two, xs, hs, wv_one, wv_two, tx_one, tx_two, near_one,
                 near_two, rp_one, rp_two, home, ys, tail, w_sem, dist_send, dist_recv, fwd_send, inc_sem, gain_send, gain_recv, halo_sem,
                 st_sem, red_send, red_recv, tail_sem):
    T, C, Q, B, F, R, KS, CL, span = dims
    FR = F * R
    pairs = T // 2
    g, z, c, s = (lax.axis_index(a) for a in ("groups", "tile", "chan", "sub"))
    sib = 1 - s
    source = z // Q
    block, odd = z // 2, lax.rem(z, 2)
    partner = z + 1 - 2 * odd
    size = CH // GROUPS

    loads = [
        pltpu.make_async_copy(w_one, wv_one, w_sem.at[0]),
        pltpu.make_async_copy(w_two, wv_two, w_sem.at[1]),
    ]
    for load in loads:
        load.start()

    def remote(src, dst, send, recv, where):
        return pltpu.make_async_remote_copy(
            src_ref=src, dst_ref=dst, send_sem=send, recv_sem=recv, device_id=where, device_id_type=MESH
        )

    barrier = pltpu.get_barrier_semaphore()
    for zz in range(T):
        for cc in range(C):
            @pl.when(jnp.logical_or(z != zz, c != cc))
            def _():
                pl.semaphore_signal(barrier, inc=1, device_id=(g, zz, cc, s), device_id_type=MESH)
    pl.semaphore_signal(barrier, inc=1, device_id=(g, z, c, sib), device_id_type=MESH)
    pl.semaphore_wait(barrier, T * C)

    def pieces(columns):
        return 3 if columns % 3 == 0 else 1

    def send_piece(src, rx, k, ch, finish):
        width = rx.shape[1] // pieces(rx.shape[1])
        cut = pl.ds(ch * width, width)
        for q in range(Q):
            zz = c * Q + q

            @pl.when(z != zz)
            def _():
                move = remote(
                    src.at[q, cut], rx.at[z, cut], dist_send.at[k, q, ch], dist_recv.at[k, z, ch], (g, zz, c, s)
                )
                if finish:
                    move.wait_send()
                else:
                    move.start()

            if not finish:
                @pl.when(z == zz)
                def _():
                    rx[z, cut] = src[q, cut]

    def onward(rx, k, t, off, ch):
        width = rx.shape[1] // pieces(rx.shape[1])
        part = rx.at[t, pl.ds(ch * width, width)]
        there = (g, z, lax.rem(c + off, C), s)
        return remote(part, part, fwd_send.at[k, off, t, ch], dist_recv.at[k, t, ch], there)

    def finish_parts(src, rx, k):
        for ch in range(pieces(rx.shape[1])):
            send_piece(src, rx, k, ch, True)

            @pl.when(source == c)
            def _():
                for t in range(T):
                    for off in range(1, C):
                        onward(rx, k, t, off, ch).wait_send()

    def receive_parts(src, rx, k):
        steps = [0]
        for far in range(1, T):
            steps += [far, -far]
        for ch in range(pieces(rx.shape[1])):
            for far in steps:
                t = z + far

                @pl.when(jnp.logical_and(source == c, jnp.logical_and(t >= 0, t < T)))
                def _():
                    if far != 0:
                        onward(rx, k, t, 0, ch).wait_recv()
                    for off in range(1, C):
                        onward(rx, k, t, off, ch).start()

        @pl.when(source != c)
        def _():
            for ch in range(pieces(rx.shape[1])):
                for t in range(T):
                    onward(rx, k, t, 0, ch).wait_recv()

    for ch in range(pieces(B)):
        send_piece(lat, rx_one, 0, ch, False)
    edge = remote(lat.at[:, 0:INTERSECTION], inc, inc_sem.at[0], inc_sem.at[1], (g, jnp.maximum(z - 1, 0), c, s))

    @pl.when(z > 0)
    def _():
        edge.start()

    @pl.when(z == T - 1)
    def _():
        inc[...] = jnp.zeros_like(inc)

    gx[c] = gains[...]
    for cc in range(C):
        @pl.when(c != cc)
        def _():
            remote(gains, gx.at[c], gain_send.at[cc], gain_recv.at[c], (g, z, cc, s)).start()

    hs[...] = jnp.zeros_like(hs)

    def reach_of(t):
        return 0 if t == T - 1 else reach_ref[t]

    my_reach = jnp.where(z == T - 1, 0, reach_ref[z])
    prior = jnp.where(z == 0, 0, reach_ref[jnp.maximum(z - 1, 0)])

    def valid(j, reach):
        return jnp.where(j < B + reach, 1.0, 0.0).astype(f32)

    def window_one(t, j):
        if j >= B:
            if t == T - 1:
                return jnp.zeros((FR, KS), f32)
            t, own, j, k = t + 1, t, j - B, j
            return rx_one[t, j].astype(f32) * valid(k, reach_of(own))
        return rx_one[t, j].astype(f32)

    def window_two(t, j):
        return rx_two[t, j].astype(f32)

    lanes = lax.broadcasted_iota(jnp.int32, (2 * T * R, KS), 1)

    def build(window, k, halo, st_own, st_sib):
        for p in range(pairs):
            total = jnp.zeros((F, 2 * R, KS), f32)
            square = jnp.zeros((F, 2 * R, KS), f32)
            for j in range(span):
                low = window(2 * p, j).reshape(F, R, KS)
                high = window(2 * p + 1, j).reshape(F, R, KS)
                both = jnp.concatenate([low, high], axis=1)
                total = total + both
                square = square + both * both
                xs[p, j] = both.astype(bf16)
            st_own[0, pl.ds(2 * p * R, 2 * R)] = jnp.sum(total, axis=0)
            st_own[1, pl.ds(2 * p * R, 2 * R)] = jnp.sum(square, axis=0)
        stats = remote(st_own, st_sib, st_sem.at[k, 0], st_sem.at[k, 1], (g, z, c, sib))
        stats.start()
        edges = remote(xs.at[:, :, F - 2:F], halo, halo_sem.at[k, 0], halo_sem.at[k, 1], (g, z, c, sib))

        @pl.when(s == 0)
        def _():
            edges.start()
            first = xs[:, :, 0:1]
            halo[:, :, 0:1] = first
            halo[:, :, 1:2] = first

        stats.wait()

        @pl.when(s == 0)
        def _():
            edges.wait_send()

        @pl.when(s == 1)
        def _():
            edges.wait_recv()

        sums = (st_own[...] + st_sib[...]).reshape(2 * T, R, KS)
        sums = jnp.broadcast_to(jnp.sum(sums, axis=1, keepdims=True), (2 * T, R, KS)).reshape(2 * T * R, KS)
        step = 1
        while step < size:
            sums = sums + jnp.where(
                (lanes & step) == 0, pltpu.roll(sums, KS - step, 1), pltpu.roll(sums, step, 1)
            )
            step *= 2
        gain = gx[source, lax.rem(z, Q)][k:k + 1]
        rows = lax.broadcasted_iota(jnp.int32, (1, R, KS), 1)
        not_first = (rows > 0).astype(f32)
        not_last = (rows < R - 1).astype(f32)
        for p in range(pairs):
            means, scales = [], []
            for t in (2 * p, 2 * p + 1):
                count = jnp.full((R, KS), (B + reach_of(t)), jnp.int32).astype(f32) * (2.0 * F * R * size)
                mean = sums[t * R:(t + 1) * R] / count
                var = sums[(T + t) * R:(T + t + 1) * R] / count - mean * mean
                means.append(mean)
                scales.append(lax.rsqrt(var + eps) * gain)
            mean = jnp.concatenate(means, axis=0)
            scale = jnp.concatenate(scales, axis=0)

            def column(j, carry):
                mask = jnp.concatenate(
                    [jnp.full((R, KS), valid(j, reach_of(t)), f32) for t in (2 * p, 2 * p + 1)], axis=0
                )
                value = jnp.concatenate([halo[p, j], xs[p, j]], axis=0).astype(f32)
                value = (value - mean) * scale
                value = value / (1.0 + jnp.exp(-value)) * mask
                hs[1, p, j + 1] = value.astype(bf16)
                split = value.reshape((F + 2) * 2, R, KS)
                down = pltpu.roll(split, 1, 1) * not_first
                hs[0, p, j + 1] = down.reshape(F + 2, 2 * R, KS).astype(bf16)
                up = pltpu.roll(split, R - 1, 1) * not_last
                hs[2, p, j + 1] = up.reshape(F + 2, 2 * R, KS).astype(bf16)
                return carry

            lax.fori_loop(0, span, column, 0)

    rows_m = span * F * 2 * R

    def convolve_reduce(wv, k, tx, near, rp):
        taps = [(a, b, d) for a in range(3) for b in range(3) for d in range(3)]

        def chunk(ch):
            rows = span // pieces(span) * FR
            return pl.ds(ch * rows, rows)

        def handed(p, ch):
            return remote(
                tx.at[2 * p + 1 - odd, chunk(ch)], near.at[p, chunk(ch)], red_send.at[k, p, ch],
                red_recv.at[k, p, ch], (g, partner, c, s)
            )

        def combined(p, ch):
            t = 2 * p + odd
            return remote(
                tx.at[t, chunk(ch)], rp.at[block, chunk(ch)], red_send.at[k, pairs + p, ch],
                red_recv.at[k, pairs + block, ch], (g, t, c, s)
            )

        def pair(i, carry):
            p = lax.rem(block + 1 + i, pairs)

            def patch(tap):
                a, b, d = tap
                return hs[b, p, d:d + span, a:a + F].reshape(rows_m, KS)

            acc = None
            for at in range(0, len(taps), 2):
                chosen = taps[at:at + 2]
                lhs = jnp.concatenate([patch(tap) for tap in chosen], axis=1)
                term = jnp.dot(lhs, wv[at * KS:(at + len(chosen)) * KS], preferred_element_type=f32)
                acc = term if acc is None else acc + term
            acc = acc.reshape(span * F, 2 * R, CL)
            for h in range(2):
                tx[2 * p + h] = acc[:, h * R:(h + 1) * R].reshape(span * FR, CL).astype(bf16)

            @pl.when(i < pairs - 1)
            def _():
                for ch in range(pieces(span)):
                    handed(p, ch).start()

            return carry

        lax.fori_loop(0, pairs, pair, 0)
        rp[block] = tx[z]
        for ch in range(pieces(span)):
            for i in range(pairs - 1):
                p = lax.rem(block + 1 + i, pairs)
                handed(p, ch).wait_recv()
                t = 2 * p + odd
                tx[t, chunk(ch)] = (tx[t, chunk(ch)].astype(f32) + near[p, chunk(ch)].astype(f32)).astype(bf16)
                combined(p, ch).start()
            handed(block, ch).start()

        def arrive(ch):
            handed(block, ch).wait_recv()
            for i in range(pairs - 1):
                p = lax.rem(block + 1 + i, pairs)
                remote(
                    tx.at[z, chunk(ch)], rp.at[p, chunk(ch)], red_send.at[k, pairs + p, ch],
                    red_recv.at[k, pairs + p, ch], (g, partner, c, s)
                ).wait_recv()

        def close():
            for ch in range(pieces(span)):
                for i in range(pairs):
                    p = lax.rem(block + 1 + i, pairs)
                    handed(p, ch).wait_send()
                    if i < pairs - 1:
                        combined(p, ch).wait_send()

        return arrive, close

    def summed(near, rp, j):
        total = near[block, j * FR:(j + 1) * FR].astype(f32)
        for m in range(pairs):
            total = total + rp[m, j * FR:(j + 1) * FR].astype(f32)
        return total

    receive_parts(lat, rx_one, 0)
    for cc in range(C):
        @pl.when(c != cc)
        def _():
            move = remote(gains, gx.at[cc], gain_send.at[cc], gain_recv.at[cc], (g, z, cc, s))
            move.wait_send()
            move.wait_recv()
    build(window_one, 0, halo_one, st_own_one, st_sib_one)
    loads[0].wait()
    arrive_one, close_one = convolve_reduce(wv_one, 0, tx_one, near_one, rp_one)
    third = span // pieces(span)
    for ch in range(pieces(span)):
        arrive_one(ch)
        for j in range(ch * third, (ch + 1) * third):
            row = (summed(near_one, rp_one, j) * valid(j, my_reach)).astype(bf16)
            for q in range(Q):
                home[q, j] = row[:, q * KS:(q + 1) * KS]
        send_piece(home, rx_two, 1, ch, False)
    receive_parts(home, rx_two, 1)
    build(window_two, 1, halo_two, st_own_two, st_sib_two)
    loads[1].wait()
    arrive_two, close_two = convolve_reduce(wv_two, 1, tx_two, near_two, rp_two)

    @pl.when(z > 0)
    def _():
        edge.wait_send()

    @pl.when(z < T - 1)
    def _():
        edge.wait_recv()

    finish_parts(lat, rx_one, 0)
    finish_parts(home, rx_two, 1)
    close_one()
    for ch in range(pieces(span)):
        arrive_two(ch)
    for j in range(span):
        row = summed(near_two, rp_two, j)
        for q in range(Q):
            base = lat[q, j] if j < B else inc[q, j - B]
            ys[q, j] = ((base.astype(f32) + row[:, q * KS:(q + 1) * KS]) * valid(j, my_reach)).astype(bf16)
    spill = remote(
        ys.at[:, B:span], tail, tail_sem.at[0], tail_sem.at[1], (g, jnp.minimum(z + 1, T - 1), c, s)
    )

    @pl.when(z < T - 1)
    def _():
        spill.start()

    @pl.when(z == 0)
    def _():
        tail[...] = jnp.zeros_like(tail)

    @pl.when(z > 0)
    def _():
        spill.wait_recv()

    for j in range(2 * B):
        if j < 2 * INTERSECTION:
            limit = jnp.full((FR, KS), 2 * prior, jnp.int32).astype(f32)
            spot = jnp.full((FR, KS), j + 0.5, f32)
            ramp = jnp.where(spot < limit, spot / jnp.maximum(limit, 2.0), 1.0)
            for q in range(Q):
                mixed = ys[q, j // 2].astype(f32) * ramp + tail[q, j // 2].astype(f32) * (1.0 - ramp)
                out[q, j] = mixed.astype(bf16)
        else:
            for q in range(Q):
                out[q, j] = ys[q, j // 2]

    close_two()

    @pl.when(z < T - 1)
    def _():
        spill.wait_send()


def stationary(latent, extents, gain_one, weight_one, gain_two, weight_two):
    F, R, B, CL = latent.shape
    T, C = lax.axis_size("tile"), lax.axis_size("chan")
    KS = weight_one.shape[3]
    Q = CL // KS
    span = B + INTERSECTION
    FR = F * R
    pairs = T // 2
    lat = latent.reshape(FR, B, Q, KS).transpose(2, 1, 0, 3)
    gains = jnp.stack([gain_one.reshape(Q, KS), gain_two.reshape(Q, KS)], axis=1)
    gains = jnp.pad(gains, ((0, 0), (0, 6), (0, 0)))
    taps = weight_one.shape[0] * weight_one.shape[1] * weight_one.shape[2]
    w_one = weight_one.reshape(taps * KS, CL)
    w_two = weight_two.reshape(taps * KS, CL)
    vm = pltpu.VMEM
    dma = pltpu.SemaphoreType.DMA
    scratch = [
        vm((T, B, FR, KS), bf16), vm((T, span, FR, KS), bf16), vm((Q, INTERSECTION, FR, KS), bf16),
        vm((C, Q, 8, KS), f32),
        vm((pairs, span, 2, 2 * R, KS), bf16), vm((pairs, span, 2, 2 * R, KS), bf16),
        vm((2, T * R, KS), f32), vm((2, T * R, KS), f32), vm((2, T * R, KS), f32), vm((2, T * R, KS), f32),
        vm((pairs, span, F, 2 * R, KS), bf16), vm((3, pairs, span + 2, F + 2, 2 * R, KS), bf16),
        vm(w_one.shape, bf16), vm(w_two.shape, bf16),
        vm((T, span * FR, CL), bf16), vm((T, span * FR, CL), bf16),
        vm((pairs, span * FR, CL), bf16), vm((pairs, span * FR, CL), bf16),
        vm((pairs, span * FR, CL), bf16), vm((pairs, span * FR, CL), bf16),
        vm((Q, span, FR, KS), bf16), vm((Q, span, FR, KS), bf16), vm((Q, INTERSECTION, FR, KS), bf16),
        dma((2,)), dma((2, Q, 3)), dma((2, T, 3)), dma((2, C, T, 3)), dma((2,)), dma((C,)), dma((C,)), dma((2, 2)), dma((2, 2)),
        dma((2, T, 3)), dma((2, T, 3)), dma((2,)),
    ]
    whole = pl.BlockSpec(memory_space=pltpu.VMEM)
    result = pl.pallas_call(
        functools.partial(block_kernel, (T, C, Q, B, F, R, KS, CL, span)),
        out_shape=jax.ShapeDtypeStruct((Q, 2 * B, FR, KS), bf16),
        in_specs=[pl.BlockSpec(memory_space=pltpu.SMEM), whole, whole,
                  pl.BlockSpec(memory_space=pl.ANY), pl.BlockSpec(memory_space=pl.ANY)],
        out_specs=whole,
        scratch_shapes=scratch,
        compiler_params=pltpu.CompilerParams(
            collective_id=0, has_side_effects=True, vmem_limit_bytes=60 * 1024 * 1024
        ),
    )(extents, lat, gains, w_one, w_two)
    result = result.reshape(Q, 2 * B, F, R, KS).transpose(2, 3, 1, 0, 4).reshape(F, R, 2 * B, CL)
    return jnp.repeat(result, 2, axis=1)


def choose(latent, extents, gain_one, weight_one, gain_two, weight_two):
    frames, rows, cols, chans = latent.shape
    share = weight_one.shape[3]
    fits = (
        share % 128 == 0
        and chans % share == 0
        and lax.axis_size("tile") % 2 == 0
        and lax.axis_size("sub") == 2
        and rows == 8
        and frames >= 2
        and (frames * rows) % 16 == 0
        and cols >= INTERSECTION
    )
    plan = stationary if fits else shards
    return plan(latent, extents, gain_one, weight_one, gain_two, weight_two)


def solution(mesh):
    placed = (
        P(("groups", "sub"), None, "tile", "chan"),
        P(),
        P("chan"),
        P(None, None, None, "tile", "chan"),
        P("chan"),
        P(None, None, None, "tile", "chan"),
    )
    return jax.shard_map(
        choose,
        mesh=mesh,
        in_specs=placed,
        out_specs=P(("groups", "sub"), None, "tile", "chan"),
        check_vma=False,
    )
```

```python
import functools

import jax
import jax.numpy as jnp
from jax import lax
from jax.experimental import pallas as pl
from jax.experimental.pallas import tpu as pltpu
from jax.sharding import PartitionSpec as P

CH = 512
GROUPS = 32
INTERSECTION = 4


eps = 1e-06


def shifted(array, axis, by):
    peers = lax.axis_size(axis)
    pairs = [(i, i + by) for i in range(peers) if 0 <= i + by < peers]
    return lax.ppermute(array, axis, pairs)


def convolve(inputs, kernel):
    result = lax.conv_general_dilated(
        inputs[None],
        kernel,
        (1, 1, 1),
        [(0, 0), (1, 1), (1, 1)],
        dimension_numbers=("NDHWC", "DHWIO", "NDHWC"),
        preferred_element_type=jnp.float32,
    )
    return result[0]


def group_norm(values, gain, count):
    group_size = CH // GROUPS
    grouped = values.reshape(values.shape[:-1] + (values.shape[-1] // group_size, group_size))
    totals, squares = lax.psum(
        (jnp.sum(grouped, axis=(0, 1, 2, 4)), jnp.sum(grouped * grouped, axis=(0, 1, 2, 4))), "sub"
    )
    size = count * group_size
    mean_val = totals / size
    variance = squares / size - mean_val * mean_val
    scaled = (grouped - mean_val[:, None]) * lax.rsqrt(variance + eps)[:, None]
    return scaled.reshape(values.shape) * gain


def causal_pad(values):
    earlier = shifted(values[-2:], "sub", 1)
    repeated = jnp.concatenate([values[:1], values[:1]], axis=0)
    leading = jnp.where(lax.axis_index("sub") == 0, repeated, earlier)
    return jnp.concatenate([leading, values], axis=0)


def blend_ramp(prior):
    positions = jnp.arange(2 * INTERSECTION).astype(jnp.float32) + 0.5
    limit = (2 * prior).astype(jnp.float32)[..., None]
    denom = (2 * jnp.maximum(prior, 1)).astype(jnp.float32)[..., None]
    return jnp.where(positions < limit, positions / denom, 1.0)


def channel_conv(padded_in, weight):
    full_in = lax.all_gather(padded_in, "chan", axis=3, tiled=True)
    out_count = weight.shape[4]
    share = weight.shape[3] // lax.axis_size("sub")
    portion = lax.dynamic_slice_in_dim(weight, lax.axis_index("sub") * share, share, 3)
    fetched = lax.all_gather(portion, "tile", axis=3, tiled=True)
    sectioned = fetched.reshape(3, 3, 3, lax.axis_size("tile"), 1, share, out_count)
    whole = lax.all_gather(sectioned, "sub", axis=4, tiled=True).reshape(3, 3, 3, -1, out_count)
    return convolve(full_in, whole)


def upscale(values):
    return jnp.repeat(jnp.repeat(values, 2, axis=1), 2, axis=2)


def shards(latent, extents, gain_one, weight_one, gain_two, weight_two):
    frame_count, row_count, col_count, chan_count = latent.shape
    tile_count = lax.axis_size("tile")
    place = lax.axis_index("tile")
    tile_ids = jnp.arange(tile_count, dtype=jnp.int32)
    reaches = jnp.where(tile_ids == tile_count - 1, 0, extents)
    reach = jnp.sum(jnp.where(tile_ids == place, reaches, 0))
    prior = jnp.sum(jnp.where(tile_ids == place - 1, reaches, 0))
    incoming = shifted(latent[:, :, :INTERSECTION, :], "tile", -1)
    window = jnp.concatenate([latent, incoming], axis=2)
    valid = (jnp.arange(col_count + INTERSECTION, dtype=jnp.int32) < col_count + reach).astype(
        jnp.float32
    )
    mask = valid[None, None, :, None]
    window = jnp.where(mask > 0, window, jnp.zeros_like(window))
    count = (col_count + reach).astype(jnp.float32) * (
        frame_count * lax.axis_size("sub") * row_count
    )
    source = window.astype(jnp.float32)
    hidden = (jax.nn.silu(group_norm(source, gain_one, count)) * mask).astype(jnp.bfloat16)
    first = (channel_conv(causal_pad(hidden), weight_one) * mask).astype(jnp.bfloat16)
    first = lax.optimization_barrier(first)
    hidden_two = (
        jax.nn.silu(group_norm(first.astype(jnp.float32), gain_two, count)) * mask
    ).astype(jnp.bfloat16)
    second = channel_conv(causal_pad(hidden_two), weight_two)
    result = ((source + second) * mask).astype(jnp.bfloat16)
    larger = upscale(result)
    own = larger[:, :, : 2 * col_count]
    arrived = shifted(larger[:, :, 2 * col_count :], "tile", 1)
    ramp = blend_ramp(prior)[None, None, :, None]
    head = own[:, :, : 2 * INTERSECTION].astype(jnp.float32) * ramp + arrived.astype(
        jnp.float32
    ) * (1.0 - ramp)
    return jnp.concatenate([head.astype(jnp.bfloat16), own[:, :, 2 * INTERSECTION :]], axis=2)


MESH = pl.DeviceIdType.MESH
f32 = jnp.float32
bf16 = jnp.bfloat16


def block_kernel(dims, reach_ref, lat_in, g_one, g_two, w_one, w_two, out, rx_one, rx_two, inc, lat, gains, gx, halo_one, halo_two,
                 st_own_one, st_own_two, st_sib_one, st_sib_two, xs, hs, wv_one, wv_two, tx_one, tx_two, near_one,
                 near_two, rp_one, rp_two, home, ys, tail, w_sem, dist_send, dist_recv, fwd_send, inc_sem, gain_send, gain_recv, halo_sem,
                 st_sem, red_send, red_recv, tail_sem):
    T, C, Q, B, F, R, KS, CL, span = dims
    FR = F * R
    pairs = T // 2
    g, z, c, s = (lax.axis_index(a) for a in ("groups", "tile", "chan", "sub"))
    sib = 1 - s
    source = z // Q
    block, odd = z // 2, lax.rem(z, 2)
    partner = z + 1 - 2 * odd
    size = CH // GROUPS

    loads = [
        pltpu.make_async_copy(w_one, wv_one, w_sem.at[0]),
        pltpu.make_async_copy(w_two, wv_two, w_sem.at[1]),
    ]
    for load in loads:
        load.start()

    def remote(src, dst, send, recv, where):
        return pltpu.make_async_remote_copy(
            src_ref=src, dst_ref=dst, send_sem=send, recv_sem=recv, device_id=where, device_id_type=MESH
        )

    barrier = pltpu.get_barrier_semaphore()
    for zz in range(T):
        for cc in range(C):
            @pl.when(jnp.logical_or(z != zz, c != cc))
            def _():
                pl.semaphore_signal(barrier, inc=1, device_id=(g, zz, cc, s), device_id_type=MESH)
    pl.semaphore_signal(barrier, inc=1, device_id=(g, z, c, sib), device_id_type=MESH)
    pl.semaphore_wait(barrier, T * C)

    for j in range(B):
        column = lat_in[:, j].astype(f32).reshape(FR, CL).astype(bf16)
        for q in range(Q):
            lat[q, j] = column[:, q * KS:(q + 1) * KS]

    def pieces(columns):
        return 3 if columns % 3 == 0 else 1

    def send_piece(src, rx, k, ch, finish):
        width = rx.shape[1] // pieces(rx.shape[1])
        cut = pl.ds(ch * width, width)
        for q in range(Q):
            zz = c * Q + q

            @pl.when(z != zz)
            def _():
                move = remote(
                    src.at[q, cut], rx.at[z, cut], dist_send.at[k, q, ch], dist_recv.at[k, z, ch], (g, zz, c, s)
                )
                if finish:
                    move.wait_send()
                else:
                    move.start()

            if not finish:
                @pl.when(z == zz)
                def _():
                    rx[z, cut] = src[q, cut]

    def onward(rx, k, t, off, ch):
        width = rx.shape[1] // pieces(rx.shape[1])
        part = rx.at[t, pl.ds(ch * width, width)]
        there = (g, z, lax.rem(c + off, C), s)
        return remote(part, part, fwd_send.at[k, off, t, ch], dist_recv.at[k, t, ch], there)

    def finish_parts(src, rx, k):
        for ch in range(pieces(rx.shape[1])):
            send_piece(src, rx, k, ch, True)

            @pl.when(source == c)
            def _():
                for t in range(T):
                    for off in range(1, C):
                        onward(rx, k, t, off, ch).wait_send()

    def receive_parts(src, rx, k):
        steps = [0]
        for far in range(1, T):
            steps += [far, -far]
        for ch in range(pieces(rx.shape[1])):
            for far in steps:
                t = z + far

                @pl.when(jnp.logical_and(source == c, jnp.logical_and(t >= 0, t < T)))
                def _():
                    if far != 0:
                        onward(rx, k, t, 0, ch).wait_recv()
                    for off in range(1, C):
                        onward(rx, k, t, off, ch).start()

        @pl.when(source != c)
        def _():
            for ch in range(pieces(rx.shape[1])):
                for t in range(T):
                    onward(rx, k, t, 0, ch).wait_recv()

    for ch in range(pieces(B)):
        send_piece(lat, rx_one, 0, ch, False)
    edge = remote(lat.at[:, 0:INTERSECTION], inc, inc_sem.at[0], inc_sem.at[1], (g, jnp.maximum(z - 1, 0), c, s))

    @pl.when(z > 0)
    def _():
        edge.start()

    @pl.when(z == T - 1)
    def _():
        inc[...] = jnp.zeros_like(inc)

    for q in range(Q):
        gains[q] = jnp.broadcast_to(g_one[q:q + 1], (8, KS))
        gains[q, 1:2] = g_two[q:q + 1]
    gx[c] = gains[...]
    for cc in range(C):
        @pl.when(c != cc)
        def _():
            remote(gains, gx.at[c], gain_send.at[cc], gain_recv.at[c], (g, z, cc, s)).start()

    hs[...] = jnp.zeros_like(hs)

    def reach_of(t):
        return 0 if t == T - 1 else reach_ref[t]

    my_reach = jnp.where(z == T - 1, 0, reach_ref[z])
    prior = jnp.where(z == 0, 0, reach_ref[jnp.maximum(z - 1, 0)])

    def valid(j, reach):
        return jnp.where(j < B + reach, 1.0, 0.0).astype(f32)

    def window_one(t, j):
        if j >= B:
            if t == T - 1:
                return jnp.zeros((FR, KS), f32)
            t, own, j, k = t + 1, t, j - B, j
            return rx_one[t, j].astype(f32) * valid(k, reach_of(own))
        return rx_one[t, j].astype(f32)

    def window_two(t, j):
        return rx_two[t, j].astype(f32)

    lanes = lax.broadcasted_iota(jnp.int32, (2 * T * R, KS), 1)

    def build(window, k, halo, st_own, st_sib):
        for p in range(pairs):
            total = jnp.zeros((F, 2 * R, KS), f32)
            square = jnp.zeros((F, 2 * R, KS), f32)
            for j in range(span):
                low = window(2 * p, j).reshape(F, R, KS)
                high = window(2 * p + 1, j).reshape(F, R, KS)
                both = jnp.concatenate([low, high], axis=1)
                total = total + both
                square = square + both * both
                xs[p, j] = both.astype(bf16)
            st_own[0, pl.ds(2 * p * R, 2 * R)] = jnp.sum(total, axis=0)
            st_own[1, pl.ds(2 * p * R, 2 * R)] = jnp.sum(square, axis=0)
        stats = remote(st_own, st_sib, st_sem.at[k, 0], st_sem.at[k, 1], (g, z, c, sib))
        stats.start()
        edges = remote(xs.at[:, :, F - 2:F], halo, halo_sem.at[k, 0], halo_sem.at[k, 1], (g, z, c, sib))

        @pl.when(s == 0)
        def _():
            edges.start()
            first = xs[:, :, 0:1]
            halo[:, :, 0:1] = first
            halo[:, :, 1:2] = first

        stats.wait()

        @pl.when(s == 0)
        def _():
            edges.wait_send()

        @pl.when(s == 1)
        def _():
            edges.wait_recv()

        sums = (st_own[...] + st_sib[...]).reshape(2 * T, R, KS)
        sums = jnp.broadcast_to(jnp.sum(sums, axis=1, keepdims=True), (2 * T, R, KS)).reshape(2 * T * R, KS)
        step = 1
        while step < size:
            sums = sums + jnp.where(
                (lanes & step) == 0, pltpu.roll(sums, KS - step, 1), pltpu.roll(sums, step, 1)
            )
            step *= 2
        gain = gx[source, lax.rem(z, Q)][k:k + 1]
        rows = lax.broadcasted_iota(jnp.int32, (1, R, KS), 1)
        not_first = (rows > 0).astype(f32)
        not_last = (rows < R - 1).astype(f32)
        for p in range(pairs):
            means, scales = [], []
            for t in (2 * p, 2 * p + 1):
                count = jnp.full((R, KS), (B + reach_of(t)), jnp.int32).astype(f32) * (2.0 * F * R * size)
                mean = sums[t * R:(t + 1) * R] / count
                var = sums[(T + t) * R:(T + t + 1) * R] / count - mean * mean
                means.append(mean)
                scales.append(lax.rsqrt(var + eps) * gain)
            mean = jnp.concatenate(means, axis=0)
            scale = jnp.concatenate(scales, axis=0)

            def column(j, carry):
                mask = jnp.concatenate(
                    [jnp.full((R, KS), valid(j, reach_of(t)), f32) for t in (2 * p, 2 * p + 1)], axis=0
                )
                value = jnp.concatenate([halo[p, j], xs[p, j]], axis=0).astype(f32)
                value = (value - mean) * scale
                value = value / (1.0 + jnp.exp(-value)) * mask
                hs[1, p, j + 1] = value.astype(bf16)
                split = value.reshape((F + 2) * 2, R, KS)
                down = pltpu.roll(split, 1, 1) * not_first
                hs[0, p, j + 1] = down.reshape(F + 2, 2 * R, KS).astype(bf16)
                up = pltpu.roll(split, R - 1, 1) * not_last
                hs[2, p, j + 1] = up.reshape(F + 2, 2 * R, KS).astype(bf16)
                return carry

            lax.fori_loop(0, span, column, 0, unroll=3 if span % 3 == 0 else 1)

    rows_m = span * F * 2 * R

    def convolve_reduce(wv, k, tx, near, rp):
        taps = [(a, b, d) for a in range(3) for b in range(3) for d in range(3)]

        def chunk(ch):
            rows = span // pieces(span) * FR
            return pl.ds(ch * rows, rows)

        def handed(p, ch):
            return remote(
                tx.at[2 * p + 1 - odd, chunk(ch)], near.at[p, chunk(ch)], red_send.at[k, p, ch],
                red_recv.at[k, p, ch], (g, partner, c, s)
            )

        def combined(p, ch):
            t = 2 * p + odd
            return remote(
                tx.at[t, chunk(ch)], rp.at[block, chunk(ch)], red_send.at[k, pairs + p, ch],
                red_recv.at[k, pairs + block, ch], (g, t, c, s)
            )

        def pair(i, carry):
            p = lax.rem(block + 1 + i, pairs)

            def patch(tap):
                a, b, d = tap
                return hs[b, p, d:d + span, a:a + F].reshape(rows_m, KS)

            acc = None
            for at in range(0, len(taps), 2):
                chosen = taps[at:at + 2]
                lhs = jnp.concatenate([patch(tap) for tap in chosen], axis=1)
                term = jnp.dot(lhs, wv[at * KS:(at + len(chosen)) * KS], preferred_element_type=f32)
                acc = term if acc is None else acc + term
            acc = acc.reshape(span * F, 2 * R, CL)
            for h in range(2):
                tx[2 * p + h] = acc[:, h * R:(h + 1) * R].reshape(span * FR, CL).astype(bf16)

            @pl.when(i < pairs - 1)
            def _():
                for ch in range(pieces(span)):
                    handed(p, ch).start()

            return carry

        lax.fori_loop(0, pairs, pair, 0)
        rp[block] = tx[z]
        for ch in range(pieces(span)):
            for i in range(pairs - 1):
                p = lax.rem(block + 1 + i, pairs)
                handed(p, ch).wait_recv()
                t = 2 * p + odd
                tx[t, chunk(ch)] = (tx[t, chunk(ch)].astype(f32) + near[p, chunk(ch)].astype(f32)).astype(bf16)
                combined(p, ch).start()
            handed(block, ch).start()

        def arrive(ch):
            handed(block, ch).wait_recv()
            for i in range(pairs - 1):
                p = lax.rem(block + 1 + i, pairs)
                remote(
                    tx.at[z, chunk(ch)], rp.at[p, chunk(ch)], red_send.at[k, pairs + p, ch],
                    red_recv.at[k, pairs + p, ch], (g, partner, c, s)
                ).wait_recv()

        def close():
            for ch in range(pieces(span)):
                for i in range(pairs):
                    p = lax.rem(block + 1 + i, pairs)
                    handed(p, ch).wait_send()
                    if i < pairs - 1:
                        combined(p, ch).wait_send()

        return arrive, close

    def summed(near, rp, j):
        total = near[block, j * FR:(j + 1) * FR].astype(f32)
        for m in range(pairs):
            total = total + rp[m, j * FR:(j + 1) * FR].astype(f32)
        return total

    receive_parts(lat, rx_one, 0)
    for cc in range(C):
        @pl.when(c != cc)
        def _():
            move = remote(gains, gx.at[cc], gain_send.at[cc], gain_recv.at[cc], (g, z, cc, s))
            move.wait_send()
            move.wait_recv()
    build(window_one, 0, halo_one, st_own_one, st_sib_one)
    loads[0].wait()
    arrive_one, close_one = convolve_reduce(wv_one, 0, tx_one, near_one, rp_one)
    third = span // pieces(span)
    for ch in range(pieces(span)):
        arrive_one(ch)
        for j in range(ch * third, (ch + 1) * third):
            row = (summed(near_one, rp_one, j) * valid(j, my_reach)).astype(bf16)
            for q in range(Q):
                home[q, j] = row[:, q * KS:(q + 1) * KS]
        send_piece(home, rx_two, 1, ch, False)
    receive_parts(home, rx_two, 1)
    build(window_two, 1, halo_two, st_own_two, st_sib_two)
    loads[1].wait()
    arrive_two, close_two = convolve_reduce(wv_two, 1, tx_two, near_two, rp_two)

    @pl.when(z > 0)
    def _():
        edge.wait_send()

    @pl.when(z < T - 1)
    def _():
        edge.wait_recv()

    finish_parts(lat, rx_one, 0)
    finish_parts(home, rx_two, 1)
    close_one()
    for ch in range(pieces(span)):
        arrive_two(ch)
    for j in range(span):
        row = summed(near_two, rp_two, j)
        for q in range(Q):
            base = lat[q, j] if j < B else inc[q, j - B]
            ys[q, j] = ((base.astype(f32) + row[:, q * KS:(q + 1) * KS]) * valid(j, my_reach)).astype(bf16)
    spill = remote(
        ys.at[:, B:span], tail, tail_sem.at[0], tail_sem.at[1], (g, jnp.minimum(z + 1, T - 1), c, s)
    )

    @pl.when(z < T - 1)
    def _():
        spill.start()

    @pl.when(z == 0)
    def _():
        tail[...] = jnp.zeros_like(tail)

    @pl.when(z > 0)
    def _():
        spill.wait_recv()

    for j in range(2 * B):
        if j < 2 * INTERSECTION:
            limit = jnp.full((FR, KS), 2 * prior, jnp.int32).astype(f32)
            spot = jnp.full((FR, KS), j + 0.5, f32)
            ramp = jnp.where(spot < limit, spot / jnp.maximum(limit, 2.0), 1.0)
            for q in range(Q):
                mixed = ys[q, j // 2].astype(f32) * ramp + tail[q, j // 2].astype(f32) * (1.0 - ramp)
                out[q, j] = mixed.astype(bf16)
        else:
            for q in range(Q):
                out[q, j] = ys[q, j // 2]

    close_two()

    @pl.when(z < T - 1)
    def _():
        spill.wait_send()


def stationary(latent, extents, gain_one, weight_one, gain_two, weight_two):
    F, R, B, CL = latent.shape
    T, C = lax.axis_size("tile"), lax.axis_size("chan")
    KS = weight_one.shape[3]
    Q = CL // KS
    span = B + INTERSECTION
    FR = F * R
    pairs = T // 2
    lat = latent.transpose(0, 2, 1, 3)
    taps = weight_one.shape[0] * weight_one.shape[1] * weight_one.shape[2]
    w_one = weight_one.reshape(taps * KS, CL)
    w_two = weight_two.reshape(taps * KS, CL)
    vm = pltpu.VMEM
    dma = pltpu.SemaphoreType.DMA
    scratch = [
        vm((T, B, FR, KS), bf16), vm((T, span, FR, KS), bf16), vm((Q, INTERSECTION, FR, KS), bf16),
        vm((Q, B, FR, KS), bf16), vm((Q, 8, KS), f32), vm((C, Q, 8, KS), f32),
        vm((pairs, span, 2, 2 * R, KS), bf16), vm((pairs, span, 2, 2 * R, KS), bf16),
        vm((2, T * R, KS), f32), vm((2, T * R, KS), f32), vm((2, T * R, KS), f32), vm((2, T * R, KS), f32),
        vm((pairs, span, F, 2 * R, KS), bf16), vm((3, pairs, span + 2, F + 2, 2 * R, KS), bf16),
        vm(w_one.shape, bf16), vm(w_two.shape, bf16),
        vm((T, span * FR, CL), bf16), vm((T, span * FR, CL), bf16),
        vm((pairs, span * FR, CL), bf16), vm((pairs, span * FR, CL), bf16),
        vm((pairs, span * FR, CL), bf16), vm((pairs, span * FR, CL), bf16),
        vm((Q, span, FR, KS), bf16), vm((Q, span, FR, KS), bf16), vm((Q, INTERSECTION, FR, KS), bf16),
        dma((2,)), dma((2, Q, 3)), dma((2, T, 3)), dma((2, C, T, 3)), dma((2,)), dma((C,)), dma((C,)), dma((2, 2)), dma((2, 2)),
        dma((2, T, 3)), dma((2, T, 3)), dma((2,)),
    ]
    whole = pl.BlockSpec(memory_space=pltpu.VMEM)
    result = pl.pallas_call(
        functools.partial(block_kernel, (T, C, Q, B, F, R, KS, CL, span)),
        out_shape=jax.ShapeDtypeStruct((Q, 2 * B, FR, KS), bf16),
        in_specs=[pl.BlockSpec(memory_space=pltpu.SMEM), whole, whole, whole,
                  pl.BlockSpec(memory_space=pl.ANY), pl.BlockSpec(memory_space=pl.ANY)],
        out_specs=whole,
        scratch_shapes=scratch,
        compiler_params=pltpu.CompilerParams(
            collective_id=0, has_side_effects=True, vmem_limit_bytes=60 * 1024 * 1024
        ),
    )(extents, lat, gain_one.reshape(Q, KS), gain_two.reshape(Q, KS), w_one, w_two)
    result = result.reshape(Q, 2 * B, F, R, KS).transpose(2, 3, 1, 0, 4).reshape(F, R, 2 * B, CL)
    return jnp.repeat(result, 2, axis=1)


def choose(latent, extents, gain_one, weight_one, gain_two, weight_two):
    frames, rows, cols, chans = latent.shape
    share = weight_one.shape[3]
    fits = (
        share % 128 == 0
        and chans % share == 0
        and lax.axis_size("tile") % 2 == 0
        and lax.axis_size("sub") == 2
        and rows == 8
        and frames >= 2
        and (frames * rows) % 16 == 0
        and cols >= INTERSECTION
    )
    plan = stationary if fits else shards
    return plan(latent, extents, gain_one, weight_one, gain_two, weight_two)


def solution(mesh):
    placed = (
        P(("groups", "sub"), None, "tile", "chan"),
        P(),
        P("chan"),
        P(None, None, None, "tile", "chan"),
        P("chan"),
        P(None, None, None, "tile", "chan"),
    )
    return jax.shard_map(
        choose,
        mesh=mesh,
        in_specs=placed,
        out_specs=P(("groups", "sub"), None, "tile", "chan"),
        check_vma=False,
    )
```

```python
import functools

import jax
import jax.numpy as jnp
from jax import lax
from jax.experimental import pallas as pl
from jax.experimental.pallas import tpu as pltpu
from jax.sharding import PartitionSpec as P

CH = 512
GROUPS = 32
INTERSECTION = 4


eps = 1e-06


def shifted(array, axis, by):
    peers = lax.axis_size(axis)
    pairs = [(i, i + by) for i in range(peers) if 0 <= i + by < peers]
    return lax.ppermute(array, axis, pairs)


def convolve(inputs, kernel):
    result = lax.conv_general_dilated(
        inputs[None],
        kernel,
        (1, 1, 1),
        [(0, 0), (1, 1), (1, 1)],
        dimension_numbers=("NDHWC", "DHWIO", "NDHWC"),
        preferred_element_type=jnp.float32,
    )
    return result[0]


def group_norm(values, gain, count):
    group_size = CH // GROUPS
    grouped = values.reshape(values.shape[:-1] + (values.shape[-1] // group_size, group_size))
    totals, squares = lax.psum(
        (jnp.sum(grouped, axis=(0, 1, 2, 4)), jnp.sum(grouped * grouped, axis=(0, 1, 2, 4))), "sub"
    )
    size = count * group_size
    mean_val = totals / size
    variance = squares / size - mean_val * mean_val
    scaled = (grouped - mean_val[:, None]) * lax.rsqrt(variance + eps)[:, None]
    return scaled.reshape(values.shape) * gain


def causal_pad(values):
    earlier = shifted(values[-2:], "sub", 1)
    repeated = jnp.concatenate([values[:1], values[:1]], axis=0)
    leading = jnp.where(lax.axis_index("sub") == 0, repeated, earlier)
    return jnp.concatenate([leading, values], axis=0)


def blend_ramp(prior):
    positions = jnp.arange(2 * INTERSECTION).astype(jnp.float32) + 0.5
    limit = (2 * prior).astype(jnp.float32)[..., None]
    denom = (2 * jnp.maximum(prior, 1)).astype(jnp.float32)[..., None]
    return jnp.where(positions < limit, positions / denom, 1.0)


def channel_conv(padded_in, weight):
    full_in = lax.all_gather(padded_in, "chan", axis=3, tiled=True)
    out_count = weight.shape[4]
    share = weight.shape[3] // lax.axis_size("sub")
    portion = lax.dynamic_slice_in_dim(weight, lax.axis_index("sub") * share, share, 3)
    fetched = lax.all_gather(portion, "tile", axis=3, tiled=True)
    sectioned = fetched.reshape(3, 3, 3, lax.axis_size("tile"), 1, share, out_count)
    whole = lax.all_gather(sectioned, "sub", axis=4, tiled=True).reshape(3, 3, 3, -1, out_count)
    return convolve(full_in, whole)


def upscale(values):
    return jnp.repeat(jnp.repeat(values, 2, axis=1), 2, axis=2)


def shards(latent, extents, gain_one, weight_one, gain_two, weight_two):
    frame_count, row_count, col_count, chan_count = latent.shape
    tile_count = lax.axis_size("tile")
    place = lax.axis_index("tile")
    tile_ids = jnp.arange(tile_count, dtype=jnp.int32)
    reaches = jnp.where(tile_ids == tile_count - 1, 0, extents)
    reach = jnp.sum(jnp.where(tile_ids == place, reaches, 0))
    prior = jnp.sum(jnp.where(tile_ids == place - 1, reaches, 0))
    incoming = shifted(latent[:, :, :INTERSECTION, :], "tile", -1)
    window = jnp.concatenate([latent, incoming], axis=2)
    valid = (jnp.arange(col_count + INTERSECTION, dtype=jnp.int32) < col_count + reach).astype(
        jnp.float32
    )
    mask = valid[None, None, :, None]
    window = jnp.where(mask > 0, window, jnp.zeros_like(window))
    count = (col_count + reach).astype(jnp.float32) * (
        frame_count * lax.axis_size("sub") * row_count
    )
    source = window.astype(jnp.float32)
    hidden = (jax.nn.silu(group_norm(source, gain_one, count)) * mask).astype(jnp.bfloat16)
    first = (channel_conv(causal_pad(hidden), weight_one) * mask).astype(jnp.bfloat16)
    first = lax.optimization_barrier(first)
    hidden_two = (
        jax.nn.silu(group_norm(first.astype(jnp.float32), gain_two, count)) * mask
    ).astype(jnp.bfloat16)
    second = channel_conv(causal_pad(hidden_two), weight_two)
    result = ((source + second) * mask).astype(jnp.bfloat16)
    larger = upscale(result)
    own = larger[:, :, : 2 * col_count]
    arrived = shifted(larger[:, :, 2 * col_count :], "tile", 1)
    ramp = blend_ramp(prior)[None, None, :, None]
    head = own[:, :, : 2 * INTERSECTION].astype(jnp.float32) * ramp + arrived.astype(
        jnp.float32
    ) * (1.0 - ramp)
    return jnp.concatenate([head.astype(jnp.bfloat16), own[:, :, 2 * INTERSECTION :]], axis=2)


MESH = pl.DeviceIdType.MESH
f32 = jnp.float32
bf16 = jnp.bfloat16


def block_kernel(dims, reach_ref, lat_in, g_one, g_two, w_one, w_two, out, rx_one, rx_two, inc, lat, gains, gx, halo_one, halo_two,
                 st_own_one, st_own_two, st_sib_one, st_sib_two, xs, hs, wv_one, wv_two, tx_one, tx_two, near_one,
                 near_two, rp_one, rp_two, home, ys, tail, w_sem, dist_send, dist_recv, fwd_send, inc_sem, gain_send, gain_recv, halo_sem,
                 st_sem, red_send, red_recv, tail_sem):
    T, C, Q, B, F, R, KS, CL, span = dims
    FR = F * R
    pairs = T // 2
    g, z, c, s = (lax.axis_index(a) for a in ("groups", "tile", "chan", "sub"))
    sib = 1 - s
    source = z // Q
    block, odd = z // 2, lax.rem(z, 2)
    partner = z + 1 - 2 * odd
    size = CH // GROUPS

    loads = [
        pltpu.make_async_copy(w_one, wv_one, w_sem.at[0]),
        pltpu.make_async_copy(w_two, wv_two, w_sem.at[1]),
    ]
    for load in loads:
        load.start()

    def remote(src, dst, send, recv, where):
        return pltpu.make_async_remote_copy(
            src_ref=src, dst_ref=dst, send_sem=send, recv_sem=recv, device_id=where, device_id_type=MESH
        )

    barrier = pltpu.get_barrier_semaphore()
    for zz in range(T):
        for cc in range(C):
            @pl.when(jnp.logical_or(z != zz, c != cc))
            def _():
                pl.semaphore_signal(barrier, inc=1, device_id=(g, zz, cc, s), device_id_type=MESH)
    pl.semaphore_signal(barrier, inc=1, device_id=(g, z, c, sib), device_id_type=MESH)
    pl.semaphore_wait(barrier, T * C)

    for j in range(B):
        column = lat_in[:, j].astype(f32).reshape(FR, CL).astype(bf16)
        for q in range(Q):
            lat[q, j] = column[:, q * KS:(q + 1) * KS]

    def pieces(columns):
        return 3 if columns % 3 == 0 else 1

    def send_piece(src, rx, k, ch, finish):
        width = rx.shape[1] // pieces(rx.shape[1])
        cut = pl.ds(ch * width, width)
        for q in range(Q):
            zz = c * Q + q

            @pl.when(z != zz)
            def _():
                move = remote(
                    src.at[q, cut], rx.at[z, cut], dist_send.at[k, q, ch], dist_recv.at[k, z, ch], (g, zz, c, s)
                )
                if finish:
                    move.wait_send()
                else:
                    move.start()

            if not finish:
                @pl.when(z == zz)
                def _():
                    rx[z, cut] = src[q, cut]

    def onward(rx, k, t, off, ch):
        width = rx.shape[1] // pieces(rx.shape[1])
        part = rx.at[t, pl.ds(ch * width, width)]
        there = (g, z, lax.rem(c + off, C), s)
        return remote(part, part, fwd_send.at[k, off, t, ch], dist_recv.at[k, t, ch], there)

    def finish_parts(src, rx, k):
        for ch in range(pieces(rx.shape[1])):
            send_piece(src, rx, k, ch, True)

            @pl.when(source == c)
            def _():
                for t in range(T):
                    for off in range(1, C):
                        onward(rx, k, t, off, ch).wait_send()

    def receive_parts(src, rx, k):
        steps = [0]
        for far in range(1, T):
            steps += [far, -far]
        for ch in range(pieces(rx.shape[1])):
            for far in steps:
                t = z + far

                @pl.when(jnp.logical_and(source == c, jnp.logical_and(t >= 0, t < T)))
                def _():
                    if far != 0:
                        onward(rx, k, t, 0, ch).wait_recv()
                    for off in range(1, C):
                        onward(rx, k, t, off, ch).start()

        @pl.when(source != c)
        def _():
            for ch in range(pieces(rx.shape[1])):
                for t in range(T):
                    onward(rx, k, t, 0, ch).wait_recv()

    for ch in range(pieces(B)):
        send_piece(lat, rx_one, 0, ch, False)
    edge = remote(lat.at[:, 0:INTERSECTION], inc, inc_sem.at[0], inc_sem.at[1], (g, jnp.maximum(z - 1, 0), c, s))

    @pl.when(z > 0)
    def _():
        edge.start()

    @pl.when(z == T - 1)
    def _():
        inc[...] = jnp.zeros_like(inc)

    for q in range(Q):
        gains[q] = jnp.broadcast_to(g_one[q:q + 1], (8, KS))
        gains[q, 1:2] = g_two[q:q + 1]
    gx[c] = gains[...]
    for cc in range(C):
        @pl.when(c != cc)
        def _():
            remote(gains, gx.at[c], gain_send.at[cc], gain_recv.at[c], (g, z, cc, s)).start()

    hs[...] = jnp.zeros_like(hs)

    def reach_of(t):
        return 0 if t == T - 1 else reach_ref[t]

    my_reach = jnp.where(z == T - 1, 0, reach_ref[z])
    prior = jnp.where(z == 0, 0, reach_ref[jnp.maximum(z - 1, 0)])

    def valid(j, reach):
        return jnp.where(j < B + reach, 1.0, 0.0).astype(f32)

    def window_one(t, j):
        if j >= B:
            if t == T - 1:
                return jnp.zeros((FR, KS), f32)
            t, own, j, k = t + 1, t, j - B, j
            return rx_one[t, j].astype(f32) * valid(k, reach_of(own))
        return rx_one[t, j].astype(f32)

    def window_two(t, j):
        return rx_two[t, j].astype(f32)

    lanes = lax.broadcasted_iota(jnp.int32, (2 * T * R, KS), 1)

    def build(window, k, halo, st_own, st_sib):
        for p in range(pairs):
            total = jnp.zeros((F, 2 * R, KS), f32)
            square = jnp.zeros((F, 2 * R, KS), f32)
            for j in range(span):
                low = window(2 * p, j).reshape(F, R, KS)
                high = window(2 * p + 1, j).reshape(F, R, KS)
                both = jnp.concatenate([low, high], axis=1)
                total = total + both
                square = square + both * both
                xs[p, j] = both.astype(bf16)
            st_own[0, pl.ds(2 * p * R, 2 * R)] = jnp.sum(total, axis=0)
            st_own[1, pl.ds(2 * p * R, 2 * R)] = jnp.sum(square, axis=0)
        stats = remote(st_own, st_sib, st_sem.at[k, 0], st_sem.at[k, 1], (g, z, c, sib))
        stats.start()
        edges = remote(xs.at[:, :, F - 2:F], halo, halo_sem.at[k, 0], halo_sem.at[k, 1], (g, z, c, sib))

        @pl.when(s == 0)
        def _():
            edges.start()
            first = xs[:, :, 0:1]
            halo[:, :, 0:1] = first
            halo[:, :, 1:2] = first

        stats.wait()

        @pl.when(s == 0)
        def _():
            edges.wait_send()

        @pl.when(s == 1)
        def _():
            edges.wait_recv()

        sums = (st_own[...] + st_sib[...]).reshape(2 * T, R, KS)
        sums = jnp.broadcast_to(jnp.sum(sums, axis=1, keepdims=True), (2 * T, R, KS)).reshape(2 * T * R, KS)
        step = 1
        while step < size:
            sums = sums + jnp.where(
                (lanes & step) == 0, pltpu.roll(sums, KS - step, 1), pltpu.roll(sums, step, 1)
            )
            step *= 2
        gain = gx[source, lax.rem(z, Q)][k:k + 1]
        rows = lax.broadcasted_iota(jnp.int32, (1, R, KS), 1)
        not_first = (rows > 0).astype(f32)
        not_last = (rows < R - 1).astype(f32)
        for p in range(pairs):
            means, scales = [], []
            for t in (2 * p, 2 * p + 1):
                count = jnp.full((R, KS), (B + reach_of(t)), jnp.int32).astype(f32) * (2.0 * F * R * size)
                mean = sums[t * R:(t + 1) * R] / count
                var = sums[(T + t) * R:(T + t + 1) * R] / count - mean * mean
                means.append(mean)
                scales.append(lax.rsqrt(var + eps) * gain)
            mean = jnp.concatenate(means, axis=0)
            scale = jnp.concatenate(scales, axis=0)

            def column(j, carry):
                mask = jnp.concatenate(
                    [jnp.full((R, KS), valid(j, reach_of(t)), f32) for t in (2 * p, 2 * p + 1)], axis=0
                )
                value = jnp.concatenate([halo[p, j], xs[p, j]], axis=0).astype(f32)
                value = (value - mean) * scale
                value = value / (1.0 + jnp.exp(-value)) * mask
                hs[1, p, j + 1] = value.astype(bf16)
                split = value.reshape((F + 2) * 2, R, KS)
                down = pltpu.roll(split, 1, 1) * not_first
                hs[0, p, j + 1] = down.reshape(F + 2, 2 * R, KS).astype(bf16)
                up = pltpu.roll(split, R - 1, 1) * not_last
                hs[2, p, j + 1] = up.reshape(F + 2, 2 * R, KS).astype(bf16)
                return carry

            lax.fori_loop(0, span, column, 0, unroll=True)

    rows_m = span * F * 2 * R

    def convolve_reduce(wv, k, tx, near, rp):
        taps = [(a, b, d) for a in range(3) for b in range(3) for d in range(3)]

        def chunk(ch):
            rows = span // pieces(span) * FR
            return pl.ds(ch * rows, rows)

        def handed(p, ch):
            return remote(
                tx.at[2 * p + 1 - odd, chunk(ch)], near.at[p, chunk(ch)], red_send.at[k, p, ch],
                red_recv.at[k, p, ch], (g, partner, c, s)
            )

        def combined(p, ch):
            t = 2 * p + odd
            return remote(
                tx.at[t, chunk(ch)], rp.at[block, chunk(ch)], red_send.at[k, pairs + p, ch],
                red_recv.at[k, pairs + block, ch], (g, t, c, s)
            )

        def pair(i, carry):
            p = lax.rem(block + 1 + i, pairs)

            def patch(tap):
                a, b, d = tap
                return hs[b, p, d:d + span, a:a + F].reshape(rows_m, KS)

            acc = None
            for at in range(0, len(taps), 2):
                chosen = taps[at:at + 2]
                lhs = jnp.concatenate([patch(tap) for tap in chosen], axis=1)
                term = jnp.dot(lhs, wv[at * KS:(at + len(chosen)) * KS], preferred_element_type=f32)
                acc = term if acc is None else acc + term
            acc = acc.reshape(span * F, 2 * R, CL)
            for h in range(2):
                tx[2 * p + h] = acc[:, h * R:(h + 1) * R].reshape(span * FR, CL).astype(bf16)

            @pl.when(i < pairs - 1)
            def _():
                for ch in range(pieces(span)):
                    handed(p, ch).start()

            return carry

        lax.fori_loop(0, pairs, pair, 0)
        rp[block] = tx[z]
        for ch in range(pieces(span)):
            for i in range(pairs - 1):
                p = lax.rem(block + 1 + i, pairs)
                handed(p, ch).wait_recv()
                t = 2 * p + odd
                tx[t, chunk(ch)] = (tx[t, chunk(ch)].astype(f32) + near[p, chunk(ch)].astype(f32)).astype(bf16)
                combined(p, ch).start()
            handed(block, ch).start()

        def arrive(ch):
            handed(block, ch).wait_recv()
            for i in range(pairs - 1):
                p = lax.rem(block + 1 + i, pairs)
                remote(
                    tx.at[z, chunk(ch)], rp.at[p, chunk(ch)], red_send.at[k, pairs + p, ch],
                    red_recv.at[k, pairs + p, ch], (g, partner, c, s)
                ).wait_recv()

        def close():
            for ch in range(pieces(span)):
                for i in range(pairs):
                    p = lax.rem(block + 1 + i, pairs)
                    handed(p, ch).wait_send()
                    if i < pairs - 1:
                        combined(p, ch).wait_send()

        return arrive, close

    def summed(near, rp, j):
        total = near[block, j * FR:(j + 1) * FR].astype(f32)
        for m in range(pairs):
            total = total + rp[m, j * FR:(j + 1) * FR].astype(f32)
        return total

    receive_parts(lat, rx_one, 0)
    for cc in range(C):
        @pl.when(c != cc)
        def _():
            move = remote(gains, gx.at[cc], gain_send.at[cc], gain_recv.at[cc], (g, z, cc, s))
            move.wait_send()
            move.wait_recv()
    build(window_one, 0, halo_one, st_own_one, st_sib_one)
    loads[0].wait()
    arrive_one, close_one = convolve_reduce(wv_one, 0, tx_one, near_one, rp_one)
    third = span // pieces(span)
    for ch in range(pieces(span)):
        arrive_one(ch)
        for j in range(ch * third, (ch + 1) * third):
            row = (summed(near_one, rp_one, j) * valid(j, my_reach)).astype(bf16)
            for q in range(Q):
                home[q, j] = row[:, q * KS:(q + 1) * KS]
        send_piece(home, rx_two, 1, ch, False)
    receive_parts(home, rx_two, 1)
    build(window_two, 1, halo_two, st_own_two, st_sib_two)
    loads[1].wait()
    arrive_two, close_two = convolve_reduce(wv_two, 1, tx_two, near_two, rp_two)

    @pl.when(z > 0)
    def _():
        edge.wait_send()

    @pl.when(z < T - 1)
    def _():
        edge.wait_recv()

    finish_parts(lat, rx_one, 0)
    finish_parts(home, rx_two, 1)
    close_one()
    for ch in range(pieces(span)):
        arrive_two(ch)
    for j in range(span):
        row = summed(near_two, rp_two, j)
        for q in range(Q):
            base = lat[q, j] if j < B else inc[q, j - B]
            ys[q, j] = ((base.astype(f32) + row[:, q * KS:(q + 1) * KS]) * valid(j, my_reach)).astype(bf16)
    spill = remote(
        ys.at[:, B:span], tail, tail_sem.at[0], tail_sem.at[1], (g, jnp.minimum(z + 1, T - 1), c, s)
    )

    @pl.when(z < T - 1)
    def _():
        spill.start()

    @pl.when(z == 0)
    def _():
        tail[...] = jnp.zeros_like(tail)

    @pl.when(z > 0)
    def _():
        spill.wait_recv()

    for j in range(2 * B):
        if j < 2 * INTERSECTION:
            limit = jnp.full((FR, KS), 2 * prior, jnp.int32).astype(f32)
            spot = jnp.full((FR, KS), j + 0.5, f32)
            ramp = jnp.where(spot < limit, spot / jnp.maximum(limit, 2.0), 1.0)
            for q in range(Q):
                mixed = ys[q, j // 2].astype(f32) * ramp + tail[q, j // 2].astype(f32) * (1.0 - ramp)
                out[:, j, :, q * KS:(q + 1) * KS] = mixed.reshape(F, R, KS).astype(bf16)
        else:
            for q in range(Q):
                plain = ys[q, j // 2].astype(f32).reshape(F, R, KS)
                out[:, j, :, q * KS:(q + 1) * KS] = plain.astype(bf16)

    close_two()

    @pl.when(z < T - 1)
    def _():
        spill.wait_send()


def stationary(latent, extents, gain_one, weight_one, gain_two, weight_two):
    F, R, B, CL = latent.shape
    T, C = lax.axis_size("tile"), lax.axis_size("chan")
    KS = weight_one.shape[3]
    Q = CL // KS
    span = B + INTERSECTION
    FR = F * R
    pairs = T // 2
    lat = latent.transpose(0, 2, 1, 3)
    taps = weight_one.shape[0] * weight_one.shape[1] * weight_one.shape[2]
    w_one = weight_one.reshape(taps * KS, CL)
    w_two = weight_two.reshape(taps * KS, CL)
    vm = pltpu.VMEM
    dma = pltpu.SemaphoreType.DMA
    scratch = [
        vm((T, B, FR, KS), bf16), vm((T, span, FR, KS), bf16), vm((Q, INTERSECTION, FR, KS), bf16),
        vm((Q, B, FR, KS), bf16), vm((Q, 8, KS), f32), vm((C, Q, 8, KS), f32),
        vm((pairs, span, 2, 2 * R, KS), bf16), vm((pairs, span, 2, 2 * R, KS), bf16),
        vm((2, T * R, KS), f32), vm((2, T * R, KS), f32), vm((2, T * R, KS), f32), vm((2, T * R, KS), f32),
        vm((pairs, span, F, 2 * R, KS), bf16), vm((3, pairs, span + 2, F + 2, 2 * R, KS), bf16),
        vm(w_one.shape, bf16), vm(w_two.shape, bf16),
        vm((T, span * FR, CL), bf16), vm((T, span * FR, CL), bf16),
        vm((pairs, span * FR, CL), bf16), vm((pairs, span * FR, CL), bf16),
        vm((pairs, span * FR, CL), bf16), vm((pairs, span * FR, CL), bf16),
        vm((Q, span, FR, KS), bf16), vm((Q, span, FR, KS), bf16), vm((Q, INTERSECTION, FR, KS), bf16),
        dma((2,)), dma((2, Q, 3)), dma((2, T, 3)), dma((2, C, T, 3)), dma((2,)), dma((C,)), dma((C,)), dma((2, 2)), dma((2, 2)),
        dma((2, T, 3)), dma((2, T, 3)), dma((2,)),
    ]
    whole = pl.BlockSpec(memory_space=pltpu.VMEM)
    result = pl.pallas_call(
        functools.partial(block_kernel, (T, C, Q, B, F, R, KS, CL, span)),
        out_shape=jax.ShapeDtypeStruct((F, 2 * B, R, CL), bf16),
        in_specs=[pl.BlockSpec(memory_space=pltpu.SMEM), whole, whole, whole,
                  pl.BlockSpec(memory_space=pl.ANY), pl.BlockSpec(memory_space=pl.ANY)],
        out_specs=whole,
        scratch_shapes=scratch,
        compiler_params=pltpu.CompilerParams(
            collective_id=0, has_side_effects=True, vmem_limit_bytes=60 * 1024 * 1024
        ),
    )(extents, lat, gain_one.reshape(Q, KS), gain_two.reshape(Q, KS), w_one, w_two)
    return jnp.repeat(result.transpose(0, 2, 1, 3), 2, axis=1)


def choose(latent, extents, gain_one, weight_one, gain_two, weight_two):
    frames, rows, cols, chans = latent.shape
    share = weight_one.shape[3]
    fits = (
        share % 128 == 0
        and chans % share == 0
        and lax.axis_size("tile") % 2 == 0
        and lax.axis_size("sub") == 2
        and rows == 8
        and frames >= 2
        and (frames * rows) % 16 == 0
        and cols >= INTERSECTION
    )
    plan = stationary if fits else shards
    return plan(latent, extents, gain_one, weight_one, gain_two, weight_two)


def solution(mesh):
    placed = (
        P(("groups", "sub"), None, "tile", "chan"),
        P(),
        P("chan"),
        P(None, None, None, "tile", "chan"),
        P("chan"),
        P(None, None, None, "tile", "chan"),
    )
    return jax.shard_map(
        choose,
        mesh=mesh,
        in_specs=placed,
        out_specs=P(("groups", "sub"), None, "tile", "chan"),
        check_vma=False,
    )
```
